32 devices in a mesh: dp: 8 (over z, x), mp: 4 (over y, core).
Axes of the slice: x: 2, y: 2, z: 4, core: 2. Of those that a mesh axis runs over, the one named last changes fastest.
Arguments:
- tokens: bfloat16 [8, 2048, 1024], P('dp'), may hold values from -6 to 6
- doc_lengths: int32 [8, 8], P('dp'), may hold values from 1 to 1024, 2048 in all within a row
- cotangent: bfloat16 [8, 2048, 1024], P('dp'), may hold values from -6 to 6
- norm_gain: bfloat16 [1024], P('dp'), may hold values from 0.5 to 1.5
- w_query: bfloat16 [1024, 1024], P('dp', 'mp'), may hold values from -0.1875 to 0.1875
- w_key: bfloat16 [1024, 1024], P('dp', 'mp'), may hold values from -0.1875 to 0.1875
- w_value: bfloat16 [1024, 1024], P('dp', 'mp'), may hold values from -0.1875 to 0.1875
- w_beta: bfloat16 [1024, 8], P('dp', 'mp'), may hold values from -0.1875 to 0.1875
- conv_taps: bfloat16 [8, 12, 128], P('mp', None, 'dp'), may hold values from -3 to 3
- head_gain: bfloat16 [128], P('dp'), may hold values from 0.5 to 1.5
- w_out: bfloat16 [1024, 1024], P('mp', 'dp'), may hold values from -0.1875 to 0.1875
- mlp_gain: bfloat16 [1024], P('dp'), may hold values from 0.5 to 1.5
- w_gate: bfloat16 [1024, 2816], P('dp', 'mp'), may hold values from -0.1875 to 0.1875
- w_up: bfloat16 [1024, 2816], P('dp', 'mp'), may hold values from -0.1875 to 0.1875
- w_down: bfloat16 [2816, 1024], P('mp', 'dp'), may hold values from -0.109375 to 0.109375
Outputs:
- layer_out: bfloat16 [8, 2048, 1024], P('dp')
- token_grad: float32 [8, 2048, 1024], P('dp')
- grad_norm_gain: float32 [1024], P('dp')
- grad_w_query: float32 [1024, 1024], P('dp', 'mp')
- grad_w_key: float32 [1024, 1024], P('dp', 'mp')
- grad_w_value: float32 [1024, 1024], P('dp', 'mp')
- grad_w_beta: float32 [1024, 8], P('dp', 'mp')
- grad_conv_taps: float32 [8, 12, 128], P('mp', None, 'dp')
- grad_head_gain: float32 [128], P('dp')
- grad_w_out: float32 [1024, 1024], P('mp', 'dp')
- grad_mlp_gain: float32 [1024], P('dp')
- grad_w_gate: float32 [1024, 2816], P('dp', 'mp')
- grad_w_up: float32 [1024, 2816], P('dp', 'mp')
- grad_w_down: float32 [2816, 1024], P('mp', 'dp')
The draws below stay inside these ranges and needn't reach their ends.
Inputs may be any that keep to these rules, and one draw needn't show every extreme that they name: `doc_lengths`: each row's 8 lengths sum to 2048, and in every row one of them is exactly 1024.
All inputs are finite; a program needn't handle non-finite values.
Results may differ from the reference program's by a relative error of at most 0.02.
Values may be sent and summed in bfloat16 or wider, within the bound.
No kernel may reach another device: no remote copies, remote signals or barrier semaphores. Data moves between devices by JAX's collectives and lax.ppermute only.
A program may use at most 320 MiB of HBM per device.

```python
import math
import jax
import jax.numpy as jnp
import numpy as np
from jax import lax

D = 1024
H = 8
DK = 128
FF = 2816
CONV = 4
GROUP = 64
LEN = 2048
DOCS = 8
MOST = 1024
ROWS = 8
HK = 1024


def levels(key, extent, shards, low, top_value):
    level, own = 1.0, jax.random.fold_in(key, 6)
    for position, shards_of in shards:
        heights = jnp.exp(jax.random.uniform(jax.random.fold_in(own, position), (shards_of,), jnp.float32, low / len(shards), top_value / len(shards)))
        level = level * jnp.repeat(heights, extent[position] // shards_of).reshape([-1 if axis == position else 1 for axis in range(len(extent))])
    return level


def profile(count, total, bound, skew):
    weights = [(1 << 20) // math.isqrt(standing ** skew) + 1 for standing in range(2, count + 1)]
    spare, given = total - bound - (count - 1), [1] * (count - 1)
    while spare > 0:
        candidates = [i for i in range(count - 1) if given[i] < bound]
        whole, left = sum([weights[i] for i in candidates]), spare
        for i in candidates:
            extra = min(bound - given[i], max(1, left * weights[i] // whole), spare)
            given[i] = given[i] + extra
            spare = spare - extra
    return np.array([bound] + given)


def ragged(own_key, number_of, total, limit, lean):
    if number_of == 2:
        one = jax.random.randint(own_key, (), max(1, total - limit), min(limit, total - 1) + 1)
        return jnp.stack([one, total - one])
    sizes = jnp.asarray(profile(number_of, total, limit, lean), jnp.int32)
    twos = (number_of - 1) // 2
    giver, sink = sizes[1:1 + 2 * twos:2], sizes[2:2 + 2 * twos:2]
    margin = jnp.minimum(giver - 1, limit - sink)
    moved = jax.random.randint(jax.random.fold_in(own_key, 1), (twos,), 0, 1 << 20) % (margin + 1)
    sizes = sizes.at[1:1 + 2 * twos:2].set(giver - moved).at[2:2 + 2 * twos:2].set(sink + moved)
    return sizes[jax.random.permutation(jax.random.fold_in(own_key, 2), number_of)]


def bell_draw(stream_key, dims, deviation, reach, cuts=(), kind=jnp.bfloat16):
    factor_of = levels(stream_key, dims, cuts, -0.22, 0.18) if cuts else 1.0
    values = jax.random.normal(stream_key, dims, jnp.float32) * deviation * factor_of
    return jnp.minimum(jnp.maximum(values, -reach), reach).astype(kind)


def setup_inputs(seed: int = 0) -> dict:
    seeds = jax.random.split(jax.random.key(seed), 16)
    tokens = bell_draw(seeds[0], (ROWS, LEN, D), 1.0, 6.0, ((0, 8),))
    doc_lengths = jax.vmap(lambda own: ragged(own, DOCS, LEN, MOST, 2))(jax.random.split(seeds[1], ROWS)).reshape((ROWS, DOCS)).astype(jnp.int32)
    cotangent = bell_draw(seeds[2], (ROWS, LEN, D), 1.0, 6.0, ((0, 8),))
    norm_gain = jnp.clip(1.0 + 0.1 * jax.random.normal(seeds[3], (D,), jnp.float32), 0.5, 1.5).astype(jnp.bfloat16)
    w_query = bell_draw(seeds[4], (D, HK), D ** -0.5, 0.1875, ((0, 8), (1, 4)))
    w_key = bell_draw(seeds[5], (D, HK), D ** -0.5, 0.1875, ((0, 8), (1, 4)))
    w_value = bell_draw(seeds[6], (D, HK), D ** -0.5, 0.1875, ((0, 8), (1, 4)))
    w_beta = bell_draw(seeds[7], (D, H), D ** -0.5, 0.1875, ((0, 8), (1, 4)))
    conv_taps = bell_draw(seeds[8], (H, 3 * CONV, DK), CONV ** -0.5, 3.0, ((0, 4), (2, 8)))
    head_gain = jnp.clip(1.0 + 0.1 * jax.random.normal(seeds[9], (DK,), jnp.float32), 0.5, 1.5).astype(jnp.bfloat16)
    w_out = bell_draw(seeds[10], (HK, D), HK ** -0.5, 0.1875, ((0, 4), (1, 8)))
    mlp_gain = jnp.clip(1.0 + 0.1 * jax.random.normal(seeds[11], (D,), jnp.float32), 0.5, 1.5).astype(jnp.bfloat16)
    w_gate = bell_draw(seeds[12], (D, FF), D ** -0.5, 0.1875, ((0, 8), (1, 4)))
    w_up = bell_draw(seeds[13], (D, FF), D ** -0.5, 0.1875, ((0, 8), (1, 4)))
    w_down = bell_draw(seeds[14], (FF, D), FF ** -0.5, 0.109375, ((0, 4), (1, 8)))
    return {"tokens": tokens, "doc_lengths": doc_lengths, "cotangent": cotangent, "norm_gain": norm_gain, "w_query": w_query, "w_key": w_key, "w_value": w_value, "w_beta": w_beta, "conv_taps": conv_taps, "head_gain": head_gain, "w_out": w_out, "mlp_gain": mlp_gain, "w_gate": w_gate, "w_up": w_up, "w_down": w_down}


epsilon = 1e-06
highest_precision = lax.Precision.HIGHEST

@jax.custom_vjp
def low(v):
    return lax.optimization_barrier(v.astype(jnp.bfloat16)).astype(jnp.float32)

@jax.custom_vjp
def low_back(v):
    return v

def low_keep(v):
    return (low(v), None)

def low_pass(kept, grad):
    return (grad,)

def back_keep(v):
    return (v, None)

def back_low(kept, grad):
    return (low(grad),)
low.defvjp(low_keep, low_pass)
low_back.defvjp(back_keep, back_low)

def rms_norm(values, gain):
    return values * lax.rsqrt(lax.optimization_barrier(jnp.mean(values * values, axis=-1, keepdims=True)) + epsilon) * gain

def doc_layout(lengths, length):
    places = jnp.arange(length, dtype=jnp.int32)
    doc_ends = jnp.cumsum(lengths).astype(jnp.int32)
    passed = places[:, None] >= doc_ends[None, :]
    doc_ids = lax.optimization_barrier(jnp.sum(passed.astype(jnp.int32), axis=1)).astype(jnp.int32)
    starts = lax.optimization_barrier(jnp.max(jnp.where(passed, doc_ends[None, :], 0), axis=1)).astype(jnp.int32)
    return (doc_ids, places - starts)

def short_conv(inputs, kernel, offsets):
    reach_len = kernel.shape[0]
    summed = inputs * kernel[reach_len - 1]
    for behind in range(1, reach_len):
        shifted = jnp.pad(inputs, ((behind, 0), (0, 0)))[:inputs.shape[0]]
        usable = (offsets >= behind).astype(jnp.float32)[:, None]
        summed = summed + shifted * kernel[reach_len - 1 - behind] * usable
    return summed

def mixer_inputs(query_proj, key_proj, value_proj, beta_logit, conv_taps, offsets):
    head_count, kernel_rows, head_dim = conv_taps.shape
    reach_len = kernel_rows // 3
    length = query_proj.shape[0]

    def branch(inputs, branch_id):
        kernel = conv_taps[:, branch_id * reach_len:(branch_id + 1) * reach_len, :]
        kernel = kernel.transpose(1, 0, 2).reshape(reach_len, head_count * head_dim)
        return jax.nn.silu(short_conv(inputs, kernel, offsets)).reshape(length, head_count, head_dim)
    query_conv = branch(query_proj, 0)
    query_matrix = query_conv * lax.rsqrt(lax.optimization_barrier(jnp.sum(query_conv * query_conv, axis=-1, keepdims=True)) + epsilon) * head_dim ** (-0.5)
    key_conv = branch(key_proj, 1)
    incoming_keys = key_conv * lax.rsqrt(lax.optimization_barrier(jnp.sum(key_conv * key_conv, axis=-1, keepdims=True)) + epsilon)
    values_in = branch(value_proj, 2)
    return (query_matrix, incoming_keys, values_in, jax.nn.sigmoid(beta_logit))

def group_step(running_state_value, blocks):
    query_matrix, incoming_keys, values_in, beta_rows, doc_ids, carried_state = blocks
    block_size = query_matrix.shape[0]
    order_idx = jnp.arange(block_size)
    same_doc = (doc_ids[:, None] == doc_ids[None, :]).astype(jnp.float32)
    strict_low = (order_idx[:, None] > order_idx[None, :]).astype(jnp.float32)
    incl_low = (order_idx[:, None] >= order_idx[None, :]).astype(jnp.float32)
    key_gram = jnp.einsum('ihd,jhd->hij', incoming_keys, incoming_keys, precision=highest_precision)
    beta_heads = beta_rows.T
    system = jnp.eye(block_size, dtype=jnp.float32) + strict_low * same_doc * beta_heads[:, :, None] * key_gram
    scaled_keys = (beta_rows[:, :, None] * incoming_keys).transpose(1, 0, 2)
    scaled_vals = (beta_rows[:, :, None] * values_in).transpose(1, 0, 2)
    decay_weight_block = lax.linalg.triangular_solve(system, scaled_keys, left_side=True, lower=True, unit_diagonal=True)
    update_block = lax.linalg.triangular_solve(system, scaled_vals, left_side=True, lower=True, unit_diagonal=True)
    fresh_value_rows = update_block - carried_state[None, :, None] * jnp.einsum('noj,njb->nob', decay_weight_block, running_state_value, precision=highest_precision)
    state_for_query = jnp.einsum('zmu,muj->mzj', query_matrix, running_state_value, precision=highest_precision)
    scores = jnp.einsum('ihd,jhd->hij', query_matrix, incoming_keys, precision=highest_precision) * (incl_low * same_doc)
    outputs = carried_state[None, :, None] * state_for_query + jnp.einsum('hij,hjv->hiv', scores, fresh_value_rows, precision=highest_precision)
    input_last_axis = same_doc[:, block_size - 1]
    updated_state = carried_state[block_size - 1] * running_state_value + jnp.einsum('sbf,bsx->bfx', incoming_keys * input_last_axis[:, None, None], fresh_value_rows, precision=highest_precision)
    return (updated_state, outputs.transpose(1, 0, 2))

def delta_rule(query_matrix, incoming_keys, values_in, beta_rows, doc_ids, offsets):
    length, head_count, head_dim = query_matrix.shape
    blocks_n = length // GROUP
    order_idx = jnp.arange(length, dtype=jnp.int32) % GROUP
    carried_state = (offsets > order_idx).astype(jnp.float32)

    def to_blocks(array_in):
        return array_in.reshape((blocks_n, GROUP) + array_in.shape[1:])
    start_state = jnp.zeros((head_count, head_dim, head_dim), jnp.float32)
    final_state, outputs = lax.scan(jax.checkpoint(group_step), start_state, (to_blocks(query_matrix), to_blocks(incoming_keys), to_blocks(values_in), to_blocks(beta_rows), to_blocks(doc_ids), to_blocks(carried_state)))
    return outputs.reshape(length, head_count, head_dim)

def layer_forward(tokens, doc_ids, offsets, norm_gain, w_query, w_key, w_value, w_beta, conv_taps, head_gain, w_out, mlp_gain, w_gate, w_up, w_down):
    length = tokens.shape[0]
    normed = low(rms_norm(tokens, norm_gain))
    query_proj = low_back(jnp.dot(normed, w_query, precision=highest_precision))
    key_proj = low_back(jnp.dot(normed, w_key, precision=highest_precision))
    value_proj = low_back(jnp.dot(normed, w_value, precision=highest_precision))
    beta_logit = low_back(jnp.dot(normed, w_beta, precision=highest_precision))
    query_matrix, incoming_keys, values_in, beta_rows = mixer_inputs(query_proj, key_proj, value_proj, beta_logit, conv_taps, offsets)
    query_matrix = low_back(low(query_matrix))
    incoming_keys = low_back(low(incoming_keys))
    values_in = low_back(low(values_in))
    mixed = delta_rule(query_matrix, incoming_keys, values_in, beta_rows, doc_ids, offsets)
    head_normed = low(rms_norm(mixed, head_gain)).reshape(length, -1)
    attended = low_back(jnp.dot(head_normed, w_out, precision=highest_precision))
    hidden_res = tokens + attended
    normed_two = low(rms_norm(hidden_res, mlp_gain))
    gate_vals = low_back(jnp.dot(normed_two, w_gate, precision=highest_precision))
    up_vals = low_back(jnp.dot(normed_two, w_up, precision=highest_precision))
    activated = low(jax.nn.silu(gate_vals) * up_vals)
    return hidden_res + low_back(jnp.dot(activated, w_down, precision=highest_precision))

def reference(tokens, doc_lengths, cotangent, norm_gain, w_query, w_key, w_value, w_beta, conv_taps, head_gain, w_out, mlp_gain, w_gate, w_up, w_down):
    weights = tuple((weight_item.astype(jnp.float32) for weight_item in (norm_gain, w_query, w_key, w_value, w_beta, conv_taps, head_gain, w_out, mlp_gain, w_gate, w_up, w_down)))

    def one_row(totals, row_data):
        row_tokens, row_lengths, row_cot = row_data
        doc_ids, offsets = doc_layout(row_lengths, LEN)

        def forward(inputs, *params):
            return layer_forward(inputs, doc_ids, offsets, *params)
        result, pull_back = jax.vjp(forward, row_tokens.astype(jnp.float32), *weights)
        grads = pull_back(row_cot.astype(jnp.float32))
        totals = tuple((total_item + grad_item for total_item, grad_item in zip(totals, grads[1:])))
        return (totals, (result.astype(jnp.bfloat16), grads[0]))
    zero_sums = tuple((jnp.zeros_like(weight_item) for weight_item in weights))
    totals, row_outs = lax.scan(one_row, zero_sums, (tokens, doc_lengths, cotangent))
    outputs, token_grads = row_outs
    return (outputs, token_grads, totals[0], totals[1], totals[2], totals[3], totals[4], totals[5], totals[6], totals[7], totals[8], totals[9], totals[10], totals[11])
```

```python
import functools
import jax
import jax.numpy as jnp
from jax import lax
from jax.experimental import pallas as pl
from jax.experimental.pallas import tpu as pltpu
from jax.sharding import PartitionSpec as P

BF = jnp.bfloat16
F32 = jnp.float32
EPS = 1e-06
STEP = 256
DK = 128
VMEM_LIMIT = 58 * 1024 * 1024
FF_PAD = 768
TAP_ROW = 4
HEAD_ROW = 28
CHUNKS = 2
ORDER = (1, 0)


def nn(a, b):
    return lax.dot_general(a, b, (((1,), (0,)), ((), ())), preferred_element_type=F32)


def nt(a, b):
    return lax.dot_general(a, b, (((1,), (1,)), ((), ())), preferred_element_type=F32)


def tn(a, b):
    return lax.dot_general(a, b, (((0,), (0,)), ((), ())), preferred_element_type=F32)


def hi_lo(x):
    high = x.astype(BF)
    return high, (x - high.astype(F32)).astype(BF)


def iota(shape, dim):
    return lax.broadcasted_iota(jnp.int32, shape, dim)


def sigmoid(x):
    return 1.0 / (1.0 + jnp.exp(-x))


def keep(mask, x):
    return jnp.where(mask, x, 0.0)


def doc_starts(ends_ref, places):
    begin = jnp.zeros_like(places)
    for doc in range(ends_ref.shape[0]):
        end = ends_ref[doc]
        begin = jnp.where(places >= end, end, begin)
    return begin


def doc_masks(ends_ref, base):
    rows = doc_starts(ends_ref, base + iota((STEP, DK), 0))
    cols = doc_starts(ends_ref, base + iota((8, STEP), 1))[0:1]
    last = jnp.int32(0)
    for doc in range(ends_ref.shape[0]):
        end = ends_ref[doc]
        last = jnp.where(base + STEP - 1 >= end, end, last)
    same = jnp.concatenate([rows, rows], axis=1) == cols
    return rows, same, rows < base, rows == last, (last < base).astype(F32)


def wide_masks():
    col = iota((64, STEP), 1)
    return [(col // 64 == b).astype(F32).astype(BF) for b in range(4)]


def spread(x, masks):
    return jnp.concatenate([x * m for m in masks], axis=0)


def wide_product(a_parts, b_parts):
    (ah, al), (bh, bl) = a_parts, b_parts
    both = nn(jnp.concatenate([ah, al], axis=0), bh)
    return both[:64] + both[64:] + nn(ah, bl)


def product(a, b):
    ah, al = hi_lo(a)
    bh, bl = hi_lo(b)
    rows = a.shape[0]
    both = nn(jnp.concatenate([ah, al], axis=0), bh)
    return both[:rows] + both[rows:] + nn(ah, bl)


def inverses(lows):
    masks = wide_masks()
    row = iota((64, STEP), 0)
    col = iota((64, STEP), 1)
    inner = col % 64
    quarter = col // 64
    eye = (row == inner).astype(F32)
    n = range(len(lows))

    def split(xs):
        return [hi_lo(x) for x in xs]

    def spreads(parts):
        return [(spread(h, masks), spread(l, masks)) for h, l in parts]

    def products(a, b):
        return [wide_product(a[i], b[i]) for i in n]

    wide = []
    for low in lows:
        total = keep(quarter == 0, low[0:64])
        for b in range(1, 4):
            total = total + keep(quarter == b, low[64 * b : 64 * b + 64])
        wide.append(total)
    small = [keep(row // 8 == inner // 8, w) for w in wide]
    small_p = split(small)
    power = products(small_p, spreads(small_p))
    power_p = split(power)
    power_s = spreads(power_p)
    third = products(small_p, power_s)
    fourth = products(power_p, power_s)
    first = [eye - small[i] + power[i] - third[i] for i in n]
    more = products(split(first), spreads(split(fourth)))
    inv = [first[i] + more[i] for i in n]
    for size in (8, 16, 32):
        pair = (row // (2 * size) == inner // (2 * size)) & (row // size != inner // size)
        off_p = split([keep(pair, w) for w in wide])
        inv_p = split(inv)
        mid = products(off_p, spreads(inv_p))
        more = products(inv_p, spreads(split(mid)))
        inv = [inv[i] - more[i] for i in n]
    off_p = split([keep(quarter == 0, low[64:128]) + keep(quarter == 2, low[192:256]) for low in lows])
    inv_p = split(inv)
    mid_p = split(products(off_p, spreads(inv_p)))
    blank = jnp.zeros((64, STEP), BF)

    def shifted(x):
        return jnp.concatenate([blank, x * masks[0], blank, x * masks[2]], axis=0)

    more = products(inv_p, [(shifted(h), shifted(l)) for h, l in mid_p])
    top, bottom = [], []
    for i in n:
        t, q = inv[i], more[i]
        top.append(
            jnp.concatenate(
                [keep(quarter == 0, t)[:, :128], (keep(quarter == 1, t) - keep(quarter == 0, q))[:, :128]], axis=0
            )
        )
        bottom.append(
            jnp.concatenate(
                [keep(quarter == 2, t)[:, 128:], (keep(quarter == 3, t) - keep(quarter == 2, q))[:, 128:]], axis=0
            )
        )
    mid = [product(lows[i][128:, :128], top[i]) for i in n]
    corner = [product(bottom[i], mid[i]) for i in n]
    blank = jnp.zeros((128, 128), F32)
    return [
        jnp.concatenate(
            [jnp.concatenate([top[i], blank], axis=1), jnp.concatenate([-corner[i], bottom[i]], axis=1)], axis=0
        )
        for i in n
    ]


def conv_of(buffer_ref, taps_ref, part, reach, base_row):
    branch, head = divmod(part, 2)
    lanes = slice(part * DK, (part + 1) * DK)
    first = TAP_ROW + head * 12 + branch * 4
    total = buffer_ref[base_row : base_row + STEP, lanes] * taps_ref[first + 3 : first + 4, :]
    for behind in range(1, 4):
        moved = buffer_ref[base_row - behind : base_row - behind + STEP, lanes]
        tap = first + 3 - behind
        total = total + keep(reach[behind], moved * taps_ref[tap : tap + 1, :])
    return total


def tn_product(a, b):
    ah, al = hi_lo(a)
    bh, bl = hi_lo(b)
    both = tn(ah, jnp.concatenate([bh, bl], axis=1))
    n = b.shape[1]
    return both[:, :n] + both[:, n:] + tn(al, bh)


def col_sum(x):
    return jnp.sum(x, axis=0, keepdims=True)


def whole(*shape):
    return pl.BlockSpec(shape, lambda *_: (0,) * len(shape))


def sds(shape, kind):
    return jax.ShapeDtypeStruct(shape, kind)


def params():
    return pltpu.CompilerParams(vmem_limit_bytes=VMEM_LIMIT)


def cost(micros, size=0):
    return pl.CostEstimate(flops=int(micros * 8e8), bytes_accessed=int(size), transcendentals=0)


def any_ref():
    return pl.BlockSpec(memory_space=pl.ANY)


def place_shards(own, shards, target, sems, depth):
    copies = []
    for k, shard in enumerate(shards):
        row = pl.multiple_of((own ^ k) * depth, depth)
        copies.append(pltpu.make_async_copy(shard, target.at[pl.ds(row, depth), :], sems.at[k]))
    for copy in copies:
        copy.start()
    for copy in copies:
        copy.wait()


def feature_rows(shards, depth):
    each = DK // shards
    row = iota((depth * shards, DK), 0)
    col = iota((depth * shards, DK), 1)
    inside = row % depth
    return ((inside < each) & ((row // depth) * each + inside == col)).astype(F32).astype(BF)


def mixer_fwd_kernel(*refs, first_row, shards, depth):
    step = pl.program_id(0)
    if shards:
        me_ref, ends_ref, tok_ref = refs[:3]
        shard_refs, refs = refs[3 : 3 + shards], refs[3 + shards :]
        outs, (buffer, state, sems) = refs[:15], refs[15:]
        w_ref, gain_ref, taps_ref, s_out_ref, halo_out_ref = outs[10:]
        outs = outs[:10]
    else:
        me_ref, ends_ref, tok_ref, w_ref, gain_ref, taps_ref, s_in_ref, halo_ref = refs[:8]
        outs, s_out_ref, halo_out_ref, (buffer, state) = refs[8:18], refs[18], refs[19], refs[20:]
    proj_ref, qkv_ref, beta_ref, mixed_ref, normed_ref, inv_ref, wu_ref, r_ref, pm_ref, state_ref = outs
    base = first_row + step * STEP

    @pl.when(step == 0)
    def _():
        if shards:
            place_shards(me_ref[0], shard_refs, w_ref, sems, depth)
            extra = w_ref[:, 768:896]
            pick = (iota((8, DK), 1) == iota((8, DK), 0) + 2).astype(F32).astype(BF)
            gain_ref[...] = nt(pick, extra)
            taps_ref[...] = tn(extra, feature_rows(shards, depth))[:32]
            state[...] = jnp.zeros_like(state)
            buffer[0:8, :] = jnp.zeros((8, 768), F32)
        else:
            state[...] = s_in_ref[...]
            buffer[0:8, :] = halo_ref[...]

    tok = tok_ref[...].astype(F32)
    scale = lax.rsqrt(jnp.mean(tok * tok, axis=-1, keepdims=True) + EPS)
    low_in = (tok * scale * gain_ref[0:1, :]).astype(BF)
    proj = nn(low_in, w_ref[...])
    buffer[8 : 8 + STEP, :] = proj[:, :768]
    proj_ref[...] = proj[:, :768]
    betas = sigmoid(proj[:, 768:896])
    beta_ref[...] = betas
    beta_t = betas.T
    rows, same, carry, in_last, go_on = doc_masks(ends_ref, base)
    behind = base + iota((STEP, DK), 0) - rows
    reach = [None] + [behind >= s for s in (1, 2, 3)]
    parts = []
    for part in range(6):
        pre = conv_of(buffer, taps_ref, part, reach, 8)
        act = pre * sigmoid(pre)
        if part < 4:
            norm = lax.rsqrt(jnp.sum(act * act, axis=-1, keepdims=True) + EPS)
            act = act * norm
            if part < 2:
                act = act * DK**-0.5
        parts.append(act.astype(BF))
    halo_out_ref[...] = buffer[STEP : STEP + 8, :]
    buffer[0:8, :] = buffer[STEP : STEP + 8, :]
    qkv_ref[...] = jnp.concatenate(parts, axis=1)
    at_row = iota((STEP, STEP), 0)
    at_col = iota((STEP, STEP), 1)
    strict = same & (at_row > at_col)
    lower = same & (at_row >= at_col)
    heads = range(2)
    q, k, v = parts[0:2], parts[2:4], parts[4:6]
    lows = [keep(strict, nt(k[h], k[h]) * betas[:, h : h + 1]) for h in heads]
    invs = inverses(lows)
    head_gain = taps_ref[HEAD_ROW : HEAD_ROW + 1, :]
    for h in heads:
        inv_ref[0, h] = invs[h].astype(BF)
        scaled_h, scaled_l = hi_lo(invs[h] * beta_t[h : h + 1, :])
        kv = jnp.concatenate([k[h], v[h]], axis=1)
        solved = nn(scaled_h, kv) + nn(scaled_l, kv)
        wu_ref[0, h] = solved.astype(BF)
        w = keep(carry, solved[:, :DK])
        both_h, both_l = hi_lo(jnp.concatenate([solved[:, DK:], w], axis=1))
        scores = keep(lower, nt(q[h], k[h])).astype(BF)
        inside = nn(scores, both_h)
        k_last = keep(in_last, k[h].astype(F32)).astype(BF)
        outer = tn(k_last, both_h) + tn(k_last, both_l)
        r = (keep(carry, q[h].astype(F32)) - inside[:, DK:]).astype(BF)
        r_ref[0, h] = r
        pm_ref[0, h] = outer[:, DK:]
        now = state[h]
        now_h, now_l = hi_lo(now)
        state_ref[0, h] = now_h
        out = nn(r, jnp.concatenate([now_h, now_l], axis=1))
        mixed = inside[:, :DK] + out[:, :DK] + out[:, DK:]
        state[h] = go_on * now - product(outer[:, DK:], now) + outer[:, :DK]
        lanes = slice(h * DK, (h + 1) * DK)
        mixed_ref[:, lanes] = mixed
        scale = lax.rsqrt(jnp.mean(mixed * mixed, axis=-1, keepdims=True) + EPS)
        normed_ref[:, lanes] = (mixed * scale * head_gain).astype(BF)
    s_out_ref[...] = state[...]


def mixer_fwd(me, ends, tokens, count, first_row, shards=None, w_in=None, small=None, carried=None):
    width = tokens.shape[1]
    steps = count // STEP
    start = first_row // STEP
    rows = lambda n, at=0: pl.BlockSpec((STEP, n), lambda i: (i + at, 0))
    group = lambda *s: pl.BlockSpec((1,) + s, lambda i: (i,) + (0,) * len(s))
    smem = pl.BlockSpec(memory_space=pltpu.SMEM)
    out_specs = [
        rows(768), rows(768), rows(DK), rows(256), rows(256),
        group(2, STEP, STEP), group(2, STEP, STEP), group(2, STEP, DK), group(2, DK, DK), group(2, DK, DK),
    ]
    out_shape = [
        sds((count, 768), F32), sds((count, 768), BF), sds((count, DK), F32), sds((count, 256), F32),
        sds((count, 256), BF), sds((steps, 2, STEP, STEP), BF), sds((steps, 2, STEP, STEP), BF),
        sds((steps, 2, STEP, DK), BF), sds((steps, 2, DK, DK), F32), sds((steps, 2, DK, DK), BF),
    ]
    scratch = [pltpu.VMEM((STEP + 8, 768), F32), pltpu.VMEM((2, DK, DK), F32)]
    if shards:
        args = [me, ends, tokens, *shards]
        in_specs = [smem, smem, rows(width, start)] + [any_ref()] * len(shards)
        out_specs += [whole(width, 896), whole(8, width), whole(32, DK)]
        out_shape += [sds((width, 896), BF), sds((8, width), F32), sds((32, DK), F32)]
        scratch.append(pltpu.SemaphoreType.DMA((len(shards),)))
    else:
        args = [me, ends, tokens, w_in, *small, *carried]
        in_specs = [
            smem, smem, rows(width, start), whole(width, 896), whole(8, width), whole(32, DK),
            whole(2, DK, DK), whole(8, 768),
        ]
    out_specs += [whole(2, DK, DK), whole(8, 768)]
    out_shape += [sds((2, DK, DK), F32), sds((8, 768), F32)]
    return pl.pallas_call(
        functools.partial(
            mixer_fwd_kernel, first_row=first_row, shards=len(shards) if shards else 0,
            depth=shards[0].shape[0] if shards else 0,
        ),
        grid=(steps,),
        in_specs=in_specs,
        out_specs=out_specs,
        out_shape=out_shape,
        scratch_shapes=scratch,
        compiler_params=params(),
        cost_estimate=cost(5 * steps),
    )(*args)


def mixer_bwd_kernel(*refs, first_row, steps, first, last, shards, depth):
    step = pl.program_id(0)
    (
        me_ref, ends_ref, mine_ref, theirs_ref, tok_ref, proj_ref, prev_ref, before_ref, qkv_ref, beta_ref, mixed_ref, normed_ref,
        inv_ref, wu_ref, r_ref, pm_ref, state_ref, w_ref, wo_ref, gain_ref, taps_ref,
    ) = refs[:21]
    refs = refs[21:]
    if not first:
        gw_in, gwo_in, gsmall_in, gnorm_in, ds_in_ref, halo_ref = refs[:6]
        refs = refs[6:]
    dn_mine, dn_theirs = refs[:2]
    refs = refs[2:]
    if last:
        sends, refs = refs[:shards], refs[shards:]
    else:
        out_refs, refs = refs[:6], refs[6:]
    buffer, ahead, dstate, d_att_s, gw_ref, gwo_ref, gsmall_ref, gnorm_ref = refs
    tile = steps - 1 - step
    base = first_row + tile * STEP
    half = tile // (steps // 2)
    core = me_ref[1] & 1

    @pl.when(step == 0)
    def _():
        if first:
            dstate[...] = jnp.zeros_like(dstate)
            ahead[:, 0:8, :] = jnp.zeros((3, 8, 768), F32)
            gw_ref[...] = jnp.zeros_like(gw_ref)
            gwo_ref[...] = jnp.zeros_like(gwo_ref)
            gsmall_ref[...] = jnp.zeros_like(gsmall_ref)
            gnorm_ref[...] = jnp.zeros_like(gnorm_ref)
        else:
            dstate[...] = ds_in_ref[...]
            ahead[:, 0:8, :] = halo_ref[...]
            gw_ref[...] = gw_in[...]
            gwo_ref[...] = gwo_in[...]
            gsmall_ref[...] = gsmall_in[...]
            gnorm_ref[...] = gnorm_in[...]

    @pl.when(half == core)
    def _():
        d_att_s[...] = mine_ref[...]

    @pl.when(half != core)
    def _():
        d_att_s[...] = theirs_ref[...]

    ahead[:, STEP : STEP + 8, :] = ahead[:, 0:8, :]
    d_att = d_att_s[...]
    d_head = nn(d_att, wo_ref[...])
    gwo_ref[...] += tn(d_att, normed_ref[...])
    rows, same, carry, in_last, go_on = doc_masks(ends_ref, base)
    at_row = iota((STEP, STEP), 0)
    at_col = iota((STEP, STEP), 1)
    strict = same & (at_row > at_col)
    lower = same & (at_row >= at_col)
    strict_t = same & (at_row < at_col)
    lower_t = same & (at_row <= at_col)
    betas = beta_ref[...]
    beta_t = betas.T
    heads = range(2)
    d_mixer = [None] * 6
    lane = iota((STEP, DK), 1)
    d_beta = jnp.zeros((STEP, DK), F32)
    head_gain = taps_ref[HEAD_ROW : HEAD_ROW + 1, :]
    for h in heads:
        lanes = slice(h * DK, (h + 1) * DK)
        mixed = mixed_ref[:, lanes]
        e = d_head[:, lanes]
        scale = lax.rsqrt(jnp.mean(mixed * mixed, axis=-1, keepdims=True) + EPS)
        unit = mixed * scale
        gsmall_ref[HEAD_ROW : HEAD_ROW + 1, :] += col_sum(e * unit)
        ge = e * head_gain
        d_out = (scale * (ge - unit * jnp.mean(unit * ge, axis=-1, keepdims=True))).astype(BF)
        q = qkv_ref[:, h * DK : (h + 1) * DK]
        k = qkv_ref[:, 256 + h * DK : 256 + (h + 1) * DK]
        v = qkv_ref[:, 512 + h * DK : 512 + (h + 1) * DK]
        wu = wu_ref[0, h]
        inv = inv_ref[0, h]
        r = r_ref[0, h]
        s_in = state_ref[0, h]
        beta_col = betas[:, h : h + 1]
        beta_row = beta_t[h : h + 1, :]
        dst = dstate[h]
        ds_h = dst.astype(BF)
        dstate[h] = go_on * dst - tn_product(pm_ref[0, h], dst) + tn(r, d_out)
        scores_t = keep(lower_t, nt(k, q)).astype(BF)
        k_last = keep(in_last, k.astype(F32)).astype(BF)
        d_x = nn(scores_t, d_out) + nn(k_last, ds_h)
        carried_w = keep(carry, wu[:, :DK].astype(F32)).astype(BF)
        x = (wu[:, DK:].astype(F32) - nn(carried_w, s_in)).astype(BF)
        d_xb = d_x.astype(BF)
        d_scores = keep(lower, nt(d_out, x)).astype(BF)
        d_scores_t = keep(lower_t, nt(x, d_out)).astype(BF)
        back_s = nt(jnp.concatenate([d_out, d_xb], axis=0), s_in)
        d_q = keep(carry, back_s[:STEP]) + nn(d_scores, k)
        d_k = nn(d_scores_t, q) + keep(in_last, nt(x, ds_h))
        d_w = -keep(carry, back_s[STEP:])
        z = tn(inv, jnp.concatenate([d_w.astype(BF), d_xb], axis=1))
        z_b = z.astype(BF)
        d_a = -keep(strict, nt(z_b, wu))
        d_a_t = -keep(strict_t, nt(wu, z_b))
        gram = nt(k, k)
        kv = jnp.concatenate([k, v], axis=1).astype(F32)
        d_b = jnp.sum(d_a * gram + z * kv, axis=-1, keepdims=True)
        d_g = (d_a * beta_col + d_a_t * beta_row).astype(BF)
        d_k = d_k + nn(d_g, k) + beta_col * z[:, :DK]
        d_v = beta_col * z[:, DK:]
        for place, grad in ((h, d_q), (2 + h, d_k), (4 + h, d_v)):
            d_mixer[place] = grad.astype(BF).astype(F32)
        d_beta = jnp.where(lane == h, d_b * beta_col * (1.0 - beta_col), d_beta)
    buffer[0:8, :] = jnp.where(tile == 0, before_ref[...], prev_ref[...])
    buffer[8 : 8 + STEP, :] = proj_ref[...]
    behind = base + iota((STEP, DK), 0) - rows
    reach = [None] + [behind >= s for s in (1, 2, 3)]
    d_proj = []
    for part in range(6):
        branch, head = divmod(part, 2)
        lanes = slice(part * DK, (part + 1) * DK)
        tap0 = TAP_ROW + head * 12 + branch * 4
        pre = conv_of(buffer, taps_ref, part, reach, 8)
        sig = sigmoid(pre)
        act = pre * sig
        grad = d_mixer[part]
        if part < 4:
            norm = lax.rsqrt(jnp.sum(act * act, axis=-1, keepdims=True) + EPS)
            unit = act * norm
            grad = norm * (grad - unit * jnp.sum(unit * grad, axis=-1, keepdims=True))
            if part < 2:
                grad = grad * DK**-0.5
        grad = grad * sig * (1.0 + pre * (1.0 - sig))
        d_in = grad * taps_ref[tap0 + 3 : tap0 + 4, :]
        gsmall_ref[tap0 + 3 : tap0 + 4, :] += col_sum(grad * buffer[8 : 8 + STEP, lanes])
        for s in (1, 2, 3):
            tap = tap0 + 3 - s
            masked = keep(reach[s], grad)
            gsmall_ref[tap : tap + 1, :] += col_sum(masked * buffer[8 - s : 8 - s + STEP, lanes])
            ahead[s - 1, 0:STEP, lanes] = masked
            d_in = d_in + ahead[s - 1, s : s + STEP, lanes] * taps_ref[tap : tap + 1, :]
        d_proj.append(d_in.astype(BF))
    d_proj.append(d_beta.astype(BF))
    d_proj = jnp.concatenate(d_proj, axis=1)
    tok = tok_ref[...].astype(F32)
    unit = tok * lax.rsqrt(jnp.mean(tok * tok, axis=-1, keepdims=True) + EPS)
    low_in = (unit * gain_ref[0:1, :]).astype(BF)
    gw_ref[...] += tn(low_in, d_proj)
    d_normed = nt(d_proj, w_ref[...])
    gnorm_ref[0:1, :] += col_sum(d_normed * unit)

    @pl.when(half == core)
    def _():
        dn_mine[...] = d_normed.astype(BF)

    @pl.when(half != core)
    def _():
        dn_theirs[...] = d_normed.astype(BF)

    @pl.when(step == steps - 1)
    def _():
        if last:
            small = jnp.concatenate([gsmall_ref[...], jnp.zeros((DK - 32, DK), F32)], axis=0).astype(BF)
            spot = (iota((8, DK), 1) == 2) & (iota((8, DK), 0) == 0)
            extra = nt(feature_rows(shards, depth), small)
            extra = extra + tn(gnorm_ref[...].astype(BF), spot.astype(F32).astype(BF))
            gw_ref[:, 768:896] += extra
            for k in range(shards):
                row = pl.multiple_of((me_ref[0] ^ k) * depth, depth)
                sends[k][:, 0:896] = gw_ref[pl.ds(row, depth), :].astype(BF)
                sends[k][:, 896:1152] = gwo_ref[pl.ds(row, depth), :].astype(BF)
        else:
            for out, value in zip(out_refs, (gw_ref, gwo_ref, gsmall_ref, gnorm_ref, dstate)):
                out[...] = value[...]
            out_refs[5][...] = ahead[:, 0:8, :]


def mixer_bwd(me, ends, mine, theirs, tokens, saved, w_in, wo_own, small, first_row, carried, last, shards):
    proj, qkv, betas, mixed, normed, inv, wu, r, pm, states, prev = saved
    count, width = proj.shape[0], tokens.shape[1]
    steps = count // STEP
    per_half = steps // 2
    start = first_row // STEP
    rows = lambda n, at=0: pl.BlockSpec((STEP, n), lambda i, me: (steps - 1 - i + at, 0))
    group = lambda *s: pl.BlockSpec((1,) + s, lambda i, me: (steps - 1 - i,) + (0,) * len(s))

    def half_rows(flip):
        def place(i, me):
            tile = steps - 1 - i
            half, inside = tile // per_half, tile % per_half
            wanted = (me[1] & 1) ^ flip
            return (jnp.where(half == wanted, inside, jnp.where(half > wanted, per_half - 1, 0)), 0)

        return pl.BlockSpec((STEP, width), place)

    in_specs = [
        pl.BlockSpec(memory_space=pltpu.SMEM), half_rows(0), half_rows(1), rows(width, start), rows(768),
        pl.BlockSpec((8, 768), lambda i, me: (jnp.maximum((steps - 1 - i) * (STEP // 8) - 1, 0), 0)),
        whole(8, 768), rows(768), rows(DK), rows(256), rows(256),
        group(2, STEP, STEP), group(2, STEP, STEP), group(2, STEP, DK), group(2, DK, DK), group(2, DK, DK),
        whole(width, 896), whole(width, 256), whole(8, width), whole(32, DK),
    ]
    args = [
        me, ends, mine, theirs, tokens, proj, proj, prev, qkv, betas, mixed, normed, inv, wu, r, pm, states, w_in, wo_own,
        *small,
    ]
    sums = [(width, 896), (width, 256), (32, DK), (8, width), (2, DK, DK), (3, 8, 768)]
    if carried is not None:
        args += carried
        in_specs += [whole(*s) for s in sums]
    depth = width // shards
    out_specs = [half_rows(0), half_rows(1)]
    out_shape = [sds((count // 2, width), BF)] * 2
    if last:
        out_specs += [whole(depth, 1152)] * shards
        out_shape += [sds((depth, 1152), BF)] * shards
    else:
        out_specs += [whole(*s) for s in sums]
        out_shape += [sds(s, F32) for s in sums]
    return pl.pallas_call(
        functools.partial(
            mixer_bwd_kernel, first_row=first_row, steps=steps, first=carried is None, last=last, shards=shards,
            depth=depth,
        ),
        grid_spec=pltpu.PrefetchScalarGridSpec(
            num_scalar_prefetch=1, grid=(steps,), in_specs=in_specs, out_specs=out_specs,
            scratch_shapes=[
                pltpu.VMEM((STEP + 8, 768), F32), pltpu.VMEM((3, STEP + 8, 768), F32), pltpu.VMEM((2, DK, DK), F32),
                pltpu.VMEM((STEP, width), BF), pltpu.VMEM((width, 896), F32), pltpu.VMEM((width, 256), F32),
                pltpu.VMEM((32, DK), F32), pltpu.VMEM((8, width), F32),
            ],
        ),
        out_shape=out_shape,
        compiler_params=params(),
        cost_estimate=cost(6 * steps),
    )(*args)


def mlp_kernel(*refs, steps, shards, depth, ff):
    step = pl.program_id(0)
    me_ref, tok_ref, cot_ref, gain_ref = refs[:4]
    head_refs, refs = refs[4:8], refs[8:]
    if shards:
        shard_refs, wo_refs, refs = refs[:shards], refs[shards : shards + 4], refs[shards + 4 :]
    else:
        g_ref, u_ref, d_ref, wo_ref = refs[:4]
        refs = refs[4:]
    back_mine, back_theirs, down_mine, down_theirs, res_ref, normed_ref, act_ref, dg_ref, du_ref, ggain_ref = refs[:10]
    refs = refs[10:]
    if shards:
        g_ref, u_ref, d_ref, wo_ref, own_ref, heads, raw, raw_wo, sems, wo_sems = refs
    else:
        (heads,) = refs
    own = me_ref[1]

    @pl.when(step == 0)
    def _():
        ggain_ref[...] = jnp.zeros_like(ggain_ref)
        if shards:
            copies = []
            for m in range(4):
                for k in range(shards):
                    row = pl.multiple_of((me_ref[0] ^ k) * depth, depth)
                    copies.append(
                        pltpu.make_async_copy(
                            wo_refs[m].at[pl.ds(k * depth, depth), :], raw_wo.at[own ^ m, pl.ds(row, depth), :],
                            wo_sems.at[m * shards + k],
                        )
                    )
            for copy in copies:
                copy.start()
            place_shards(me_ref[0], shard_refs, raw, sems, depth)
            inside = iota((256, FF_PAD), 1) < ff
            for at in range(0, raw.shape[0], 256):
                here = slice(at, at + 256)
                g_ref[here, :] = keep(inside, raw[here, 256 : 256 + FF_PAD].astype(F32)).astype(BF)
                from_u = 256 + ff - (256 + ff) % 128
                turned = pltpu.roll(
                    raw[here, from_u : from_u + FF_PAD].astype(F32), FF_PAD - (256 + ff) % 128, axis=1
                )
                u_ref[here, :] = keep(inside, turned).astype(BF)
                from_d = 256 + 2 * ff
                d_ref[here, :] = keep(inside, raw[here, from_d : from_d + FF_PAD].astype(F32)).astype(BF)
            for copy in copies:
                copy.wait()
            wo_ref[...] = raw_wo[...]
            own_ref[...] = raw_wo[own]

    for m in range(4):
        heads[own ^ m] = head_refs[m][...]
    attended = nt(heads[0], wo_ref[0])
    for m in range(1, 4):
        attended = attended + nt(heads[m], wo_ref[m])
    res = tok_ref[...].astype(F32) + attended
    unit = res * lax.rsqrt(jnp.mean(res * res, axis=-1, keepdims=True) + EPS)
    normed = (unit * gain_ref[1:2, :]).astype(BF)
    normed_ref[...] = normed
    gate = nn(normed, g_ref[...])
    up = nn(normed, u_ref[...])
    sig = sigmoid(gate)
    silu = gate * sig
    act = (silu * up).astype(BF)
    act_ref[...] = act
    d_hidden = nn(cot_ref[...], d_ref[...])
    d_gate = (d_hidden * up * sig * (1.0 + gate * (1.0 - sig))).astype(BF)
    d_up = (d_hidden * silu).astype(BF)
    dg_ref[...] = d_gate
    du_ref[...] = d_up
    down = nt(act, d_ref[...]).astype(BF)
    back = nt(d_gate, g_ref[...]) + nt(d_up, u_ref[...])
    ggain_ref[0:1, :] += col_sum(back * unit)

    @pl.when(step < steps // 2)
    def _():
        back_theirs[...] = back.astype(BF)
        down_theirs[...] = down

    @pl.when(step >= steps // 2)
    def _():
        back_mine[...] = back.astype(BF)
        down_mine[...] = down
        res_ref[...] = res


def mlp(me, tokens, cot, small, heads, count, first_row, ff, shards=None, wo=None, weights=None):
    width = tokens.shape[1]
    steps = count // STEP
    per_half = steps // 2
    start = first_row // STEP

    def tile(i, me, at=0):
        half = jnp.where(i >= per_half, me[1] & 1, 1 - (me[1] & 1))
        return at + half * per_half + i % per_half

    rows = lambda n, at=0: pl.BlockSpec((STEP, n), lambda i, me: (tile(i, me, at), 0))
    theirs = pl.BlockSpec((STEP, width), lambda i, me: (jnp.minimum(i, per_half - 1), 0))
    mine = pl.BlockSpec((STEP, width), lambda i, me: (jnp.maximum(i - per_half, 0), 0))
    in_specs = [rows(width, start), rows(width, start), whole(8, width)] + [rows(256)] * 4
    args = [me, tokens, cot, small[0], *heads]
    out_specs = [mine, theirs, mine, theirs, mine, rows(width), rows(FF_PAD), rows(FF_PAD), rows(FF_PAD), whole(8, width)]
    halves = (count // 2, width)
    out_shape = [
        sds(halves, BF), sds(halves, BF), sds(halves, BF), sds(halves, BF), sds(halves, F32), sds((count, width), BF),
        sds((count, FF_PAD), BF), sds((count, FF_PAD), BF), sds((count, FF_PAD), BF), sds((8, width), F32),
    ]
    kept = [(width, FF_PAD)] * 3 + [(4, width, 256)]
    scratch = [pltpu.VMEM((4, STEP, 256), BF)]
    if shards:
        in_specs += [any_ref()] * (len(shards) + 4)
        args += [*shards, *wo]
        out_specs += [whole(*s) for s in kept] + [whole(width, 256)]
        out_shape += [sds(s, BF) for s in kept] + [sds((width, 256), BF)]
        scratch += [
            pltpu.VMEM((width, shards[0].shape[1]), BF), pltpu.VMEM((4, width, 256), BF),
            pltpu.SemaphoreType.DMA((len(shards),)), pltpu.SemaphoreType.DMA((4 * len(shards),)),
        ]
    else:
        in_specs += [whole(*s) for s in kept]
        args += weights
    return pl.pallas_call(
        functools.partial(
            mlp_kernel, steps=steps, shards=len(shards) if shards else 0, depth=shards[0].shape[0] if shards else 0,
            ff=ff,
        ),
        grid_spec=pltpu.PrefetchScalarGridSpec(
            num_scalar_prefetch=1, grid=(steps,), in_specs=in_specs, out_specs=out_specs, scratch_shapes=scratch,
        ),
        out_shape=out_shape,
        compiler_params=params(),
        cost_estimate=cost(3.2 * steps),
    )(*args)


def mlp_grads_kernel(me_ref, *refs, chunks, shards, depth, ff):
    step = pl.program_id(0)
    normed, cot, dg, du, act = (refs[i * chunks : (i + 1) * chunks] for i in range(5))
    gain_ref = refs[5 * chunks]
    sends, packed = refs[5 * chunks + 1 : -1], refs[-1]
    each = 256 // depth

    def over_rows(left, right):
        total = tn(left[0][...], right[0][...])
        for a, b in zip(left[1:], right[1:]):
            total = total + tn(a[...], b[...])
        return total

    g_gate = over_rows(normed, dg)
    g_up = over_rows(normed, du)
    g_down = over_rows(cot, act)
    spot = (iota((8, FF_PAD), 1) == ff) & (iota((8, FF_PAD), 0) == 0)
    g_down = g_down + tn(gain_ref[...].astype(BF), spot.astype(F32).astype(BF))
    cut = ff - ff % 128
    turned = pltpu.roll(g_up, ff % 128, axis=1)
    packed[:, 0:cut] = g_gate[:, 0:cut]
    packed[:, cut : cut + 128] = g_gate[:, cut : cut + 128] + turned[:, 0:128]
    packed[:, cut + 128 : 2 * ff] = turned[:, 128 : 2 * ff - cut]
    packed[:, 2 * ff : 2 * ff + FF_PAD] = g_down
    for i in range(len(sends) // each):

        @pl.when(step == i)
        def _(i=i):
            for t in range(each):
                row = pl.multiple_of((t ^ (me_ref[0] % each)) * depth, depth)
                sends[i * each + t][...] = packed[pl.ds(row, depth), :].astype(BF)


def mlp_grads(me, normed, cot, dg, du, act, gain, shards, ff):
    chunks = len(normed)
    count, width = normed[0].shape
    depth = width // shards
    each = 256 // depth
    block = lambda i, me: (me[0] // each) ^ i
    column = lambda at=0: pl.BlockSpec((count, 256), lambda i, me: (at, block(i, me)))
    wide = 2 * ff + FF_PAD
    return pl.pallas_call(
        functools.partial(mlp_grads_kernel, chunks=chunks, shards=shards, depth=depth, ff=ff),
        grid_spec=pltpu.PrefetchScalarGridSpec(
            num_scalar_prefetch=1,
            grid=(width // 256,),
            in_specs=[column()] * chunks
            + [column(c) for c in range(chunks)]
            + [whole(count, FF_PAD)] * (3 * chunks)
            + [pl.BlockSpec((8, 256), lambda i, me: (0, block(i, me)))],
            out_specs=[whole(depth, wide)] * shards,
            scratch_shapes=[pltpu.VMEM((256, wide), F32)],
        ),
        out_shape=[sds((depth, wide), BF)] * shards,
        compiler_params=params(),
        cost_estimate=cost(12),
    )(me, *normed, *([cot] * chunks), *dg, *du, *act, gain)


def norm_back(e, v, gain):
    scale = lax.rsqrt(jnp.mean(v * v, axis=-1, keepdims=True) + EPS)
    unit = v * scale
    ge = e * gain
    return scale * (ge - unit * jnp.mean(unit * ge, axis=-1, keepdims=True))


def resid_kernel(me_ref, p_ref, q_ref, res_ref, cot_ref, gain_ref, d_resid_ref, d_att_ref):
    e = p_ref[...].astype(F32) + q_ref[...].astype(F32)
    d_resid = cot_ref[...].astype(F32) + norm_back(e, res_ref[...], gain_ref[1:2, :])
    d_resid_ref[...] = d_resid
    d_att_ref[...] = d_resid.astype(BF)


def token_kernel(me_ref, p_ref, q_ref, d_resid_ref, tok_ref, gain_ref, out_ref):
    e = p_ref[...].astype(F32) + q_ref[...].astype(F32)
    out_ref[...] = (d_resid_ref[...] + norm_back(e, tok_ref[...].astype(F32), gain_ref[0:1, :])).astype(BF)


def half_call(kernel, me, arrays, full, gain, first_row, outs):
    count, width = arrays[0].shape
    tiles = count // STEP
    start = first_row // STEP
    rows = pl.BlockSpec((STEP, width), lambda i, me: (i, 0))
    out_shape = [sds((count, width), kind) for kind in outs]
    return pl.pallas_call(
        kernel,
        grid_spec=pltpu.PrefetchScalarGridSpec(
            num_scalar_prefetch=1,
            grid=(tiles,),
            in_specs=[rows] * len(arrays)
            + [pl.BlockSpec((STEP, width), lambda i, me: (start + (me[1] & 1) * tiles + i, 0)), whole(8, width)],
            out_specs=[rows] * len(outs),
        ),
        out_shape=out_shape,
        compiler_params=params(),
        cost_estimate=cost(1.5),
    )(me, *arrays, full, gain)


def swap(x, axis, k):
    return lax.ppermute(x, axis, [(i, i ^ k) for i in range(lax.axis_size(axis))])


def pair_sum(own, other):
    return (own.astype(F32) + other.astype(F32)).astype(BF)


def on_device(
    tokens, doc_lengths, cotangent, norm_gain, w_query, w_key, w_value, w_beta, conv_taps, head_gain, w_out, mlp_gain,
    w_gate, w_up, w_down,
):
    seq_rows, length, width = tokens.shape
    shards = lax.axis_size("dp")
    depth = width // shards
    each = conv_taps.shape[2]
    ff = w_gate.shape[1]
    me = jnp.stack([lax.axis_index("dp"), lax.axis_index("mp")]).astype(jnp.int32)
    ends = jnp.cumsum(doc_lengths[0]).astype(jnp.int32)
    flat = tokens.reshape(length, width)
    cot = cotangent.reshape(length, width)
    tall = lambda x: jnp.pad(x, ((0, depth - x.shape[0]), (0, 0)))
    pack = jnp.concatenate(
        [
            w_query, w_key, w_value, w_beta, norm_gain[:, None], mlp_gain[:, None],
            tall(conv_taps.reshape(24, each).T), tall(head_gain[:, None]), jnp.zeros((depth, 99), BF),
        ],
        axis=1,
    )
    mixer_shards = [pack] + [swap(pack, "dp", k) for k in range(1, shards)]
    pack_two = jnp.concatenate(
        [w_out.T, w_gate, w_up, w_down.T, jnp.zeros((depth, FF_PAD - ff), BF)], axis=1
    )
    count = length // CHUNKS
    fwd, carried, w_in, small = [], None, None, None
    for c in range(CHUNKS):
        if c == 0:
            out = mixer_fwd(me, ends, flat, count, 0, shards=mixer_shards)
            w_in, small = out[10], (out[11], out[12])
            carried = out[13:]
            prev = jnp.zeros((8, 768), F32)
        else:
            out = mixer_fwd(me, ends, flat, count, c * count, w_in=w_in, small=small, carried=carried)
            prev = carried[1]
            carried = out[10:]
        fwd.append(list(out[:10]) + [prev])
    mlp_shards = [pack_two]
    far = [swap(pack_two, "dp", k) for k in range(2, shards, 2)]
    near = [swap(x, "dp", 1) for x in [pack_two] + far]
    mlp_shards = [x for pair in zip([pack_two] + far, near) for x in pair]
    wo_own = jnp.concatenate([x[:, :256] for x in mlp_shards], axis=0)
    wo_y = swap(wo_own, "mp", 2)
    wo = [wo_own, swap(wo_own, "mp", 1), wo_y, swap(wo_y, "mp", 1)]
    heads = []
    for c in range(CHUNKS):
        own = fwd[c][4]
        far_heads = swap(own, "mp", 2)
        heads.append([own, swap(own, "mp", 1), far_heads, swap(far_heads, "mp", 1)])
    order = ORDER
    mid, weights, own_wo = [None] * CHUNKS, None, None
    for c in order:
        if weights is None:
            out = mlp(me, flat, cot, small, heads[c], count, c * count, ff, shards=mlp_shards, wo=wo)
            weights, own_wo = list(out[10:14]), out[14]
        else:
            out = mlp(me, flat, cot, small, heads[c], count, c * count, ff, weights=weights)
        mid[c] = out
    resid = [None] * CHUNKS
    for c in order:
        p = pair_sum(mid[c][0], swap(mid[c][1], "mp", 1))
        q = swap(p, "mp", 2)
        d_resid, d_att = half_call(resid_kernel, me, [p, q, mid[c][4]], cot, small[0], c * count, [F32, BF])
        resid[c] = (d_resid, d_att, swap(d_att, "mp", 1))
    ggain = sum(mid[c][9] for c in range(CHUNKS))
    sends = mlp_grads(
        me, [m[5] for m in mid], cot, [m[7] for m in mid], [m[8] for m in mid], [m[6] for m in mid], ggain, shards, ff
    )
    mlp_sum = sum(swap(sends[k], "dp", k).astype(F32) if k else sends[0].astype(F32) for k in range(shards))
    layer = [None] * CHUNKS
    for c in order:
        p = pair_sum(mid[c][2], swap(mid[c][3], "mp", 1))
        q = swap(p, "mp", 2)
        mine = (mid[c][4] + (p.astype(F32) + q.astype(F32))).astype(BF)
        layer[c] = (mine, swap(mine, "mp", 1))
    carried, token_halves = None, [None] * CHUNKS
    for c in reversed(range(CHUNKS)):
        d_resid, d_att, d_att_other = resid[c]
        out = mixer_bwd(
            me, ends, d_att, d_att_other, flat, fwd[c], w_in, own_wo, small, c * count, carried, c == 0, shards
        )
        carried = list(out[2:])
        p = pair_sum(out[0], swap(out[1], "mp", 1))
        q = swap(p, "mp", 2)
        (mine,) = half_call(token_kernel, me, [p, q, d_resid], flat, small[0], c * count, [BF])
        token_halves[c] = (mine, swap(mine, "mp", 1))
    mix_sum = sum(swap(carried[k], "dp", k).astype(F32) if k else carried[0].astype(F32) for k in range(shards))
    low_core = (me[1] & 1) == 0

    def join(halves):
        parts = []
        for mine, other in halves:
            parts += [jnp.where(low_core, mine, other), jnp.where(low_core, other, mine)]
        return jnp.concatenate(parts, axis=0)

    layer_out = join(layer).reshape(seq_rows, length, width)
    token_grad = join(token_halves).astype(F32).reshape(seq_rows, length, width)
    extra = mix_sum[:, 768:896]
    gains = jnp.concatenate([extra[:, 2], mlp_sum[:, 3 * ff], extra[:each, 28]])
    gains = gains + swap(gains, "mp", 1)
    gains = gains + swap(gains, "mp", 2)
    return (
        layer_out,
        token_grad,
        gains[:depth],
        mix_sum[:, 0:256],
        mix_sum[:, 256:512],
        mix_sum[:, 512:768],
        extra[:, 0:2],
        extra[:each, 4:28].T.reshape(2, 12, each),
        gains[2 * depth :],
        mix_sum[:, 896:1152].T,
        gains[depth : 2 * depth],
        mlp_sum[:, 0:ff],
        mlp_sum[:, ff : 2 * ff],
        mlp_sum[:, 2 * ff : 3 * ff].T,
    )


def solution(mesh):
    return jax.shard_map(
        on_device,
        mesh=mesh,
        in_specs=(
            P("dp", None, None),
            P("dp", None),
            P("dp", None, None),
            P("dp"),
            P("dp", "mp"),
            P("dp", "mp"),
            P("dp", "mp"),
            P("dp", "mp"),
            P("mp", None, "dp"),
            P("dp"),
            P("mp", "dp"),
            P("dp"),
            P("dp", "mp"),
            P("dp", "mp"),
            P("mp", "dp"),
        ),
        out_specs=(
            P("dp", None, None),
            P("dp", None, None),
            P("dp"),
            P("dp", "mp"),
            P("dp", "mp"),
            P("dp", "mp"),
            P("dp", "mp"),
            P("mp", None, "dp"),
            P("dp"),
            P("mp", "dp"),
            P("dp"),
            P("dp", "mp"),
            P("dp", "mp"),
            P("mp", "dp"),
        ),
        check_vma=False,
    )
```

```python
import functools
import jax
import jax.numpy as jnp
from jax import lax
from jax.experimental import pallas as pl
from jax.experimental.pallas import tpu as pltpu
from jax.sharding import PartitionSpec as P

BF = jnp.bfloat16
F32 = jnp.float32
EPS = 1e-06
STEP = 256
DK = 128
VMEM_LIMIT = 58 * 1024 * 1024
FF_PAD = 768
TAP_ROW = 4
HEAD_ROW = 28
CHUNKS = 2
ORDER = (1, 0)
TILE = 512
COST = 1.0


def nn(a, b):
    return lax.dot_general(a, b, (((1,), (0,)), ((), ())), preferred_element_type=F32)


def nt(a, b):
    return lax.dot_general(a, b, (((1,), (1,)), ((), ())), preferred_element_type=F32)


def tn(a, b):
    return lax.dot_general(a, b, (((0,), (0,)), ((), ())), preferred_element_type=F32)


def hi_lo(x):
    high = x.astype(BF)
    return high, (x - high.astype(F32)).astype(BF)


def iota(shape, dim):
    return lax.broadcasted_iota(jnp.int32, shape, dim)


def sigmoid(x):
    return 1.0 / (1.0 + jnp.exp(-x))


def keep(mask, x):
    return jnp.where(mask, x, 0.0)


def doc_starts(ends_ref, places):
    begin = jnp.zeros_like(places)
    for doc in range(ends_ref.shape[0]):
        end = ends_ref[doc]
        begin = jnp.where(places >= end, end, begin)
    return begin


def doc_masks(ends_ref, base):
    rows = doc_starts(ends_ref, base + iota((STEP, DK), 0))
    cols = doc_starts(ends_ref, base + iota((8, STEP), 1))[0:1]
    last = jnp.int32(0)
    for doc in range(ends_ref.shape[0]):
        end = ends_ref[doc]
        last = jnp.where(base + STEP - 1 >= end, end, last)
    same = jnp.concatenate([rows, rows], axis=1) == cols
    return rows, same, rows < base, rows == last, (last < base).astype(F32)


def wide_masks():
    col = iota((64, STEP), 1)
    return [(col // 64 == b).astype(F32).astype(BF) for b in range(4)]


def spread(x, masks):
    return jnp.concatenate([x * m for m in masks], axis=0)


def wide_product(a_parts, b_parts):
    (ah, al), (bh, bl) = a_parts, b_parts
    both = nn(jnp.concatenate([ah, al], axis=0), bh)
    return both[:64] + both[64:] + nn(ah, bl)


def product(a, b):
    ah, al = hi_lo(a)
    bh, bl = hi_lo(b)
    rows = a.shape[0]
    both = nn(jnp.concatenate([ah, al], axis=0), bh)
    return both[:rows] + both[rows:] + nn(ah, bl)


def inverses(lows):
    masks = wide_masks()
    row = iota((64, STEP), 0)
    col = iota((64, STEP), 1)
    inner = col % 64
    quarter = col // 64
    eye = (row == inner).astype(F32)
    n = range(len(lows))

    def split(xs):
        return [hi_lo(x) for x in xs]

    def spreads(parts):
        return [(spread(h, masks), spread(l, masks)) for h, l in parts]

    def products(a, b):
        return [wide_product(a[i], b[i]) for i in n]

    wide = []
    for low in lows:
        total = keep(quarter == 0, low[0:64])
        for b in range(1, 4):
            total = total + keep(quarter == b, low[64 * b : 64 * b + 64])
        wide.append(total)
    small = [keep(row // 8 == inner // 8, w) for w in wide]
    small_p = split(small)
    power = products(small_p, spreads(small_p))
    power_p = split(power)
    power_s = spreads(power_p)
    third = products(small_p, power_s)
    fourth = products(power_p, power_s)
    first = [eye - small[i] + power[i] - third[i] for i in n]
    more = products(split(first), spreads(split(fourth)))
    inv = [first[i] + more[i] for i in n]
    for size in (8, 16, 32):
        pair = (row // (2 * size) == inner // (2 * size)) & (row // size != inner // size)
        off_p = split([keep(pair, w) for w in wide])
        inv_p = split(inv)
        mid = products(off_p, spreads(inv_p))
        more = products(inv_p, spreads(split(mid)))
        inv = [inv[i] - more[i] for i in n]
    off_p = split([keep(quarter == 0, low[64:128]) + keep(quarter == 2, low[192:256]) for low in lows])
    inv_p = split(inv)
    mid_p = split(products(off_p, spreads(inv_p)))
    blank = jnp.zeros((64, STEP), BF)

    def shifted(x):
        return jnp.concatenate([blank, x * masks[0], blank, x * masks[2]], axis=0)

    more = products(inv_p, [(shifted(h), shifted(l)) for h, l in mid_p])
    top, bottom = [], []
    for i in n:
        t, q = inv[i], more[i]
        top.append(
            jnp.concatenate(
                [keep(quarter == 0, t)[:, :128], (keep(quarter == 1, t) - keep(quarter == 0, q))[:, :128]], axis=0
            )
        )
        bottom.append(
            jnp.concatenate(
                [keep(quarter == 2, t)[:, 128:], (keep(quarter == 3, t) - keep(quarter == 2, q))[:, 128:]], axis=0
            )
        )
    mid = [product(lows[i][128:, :128], top[i]) for i in n]
    corner = [product(bottom[i], mid[i]) for i in n]
    blank = jnp.zeros((128, 128), F32)
    return [
        jnp.concatenate(
            [jnp.concatenate([top[i], blank], axis=1), jnp.concatenate([-corner[i], bottom[i]], axis=1)], axis=0
        )
        for i in n
    ]


def conv_of(buffer_ref, taps_ref, part, reach, base_row):
    branch, head = divmod(part, 2)
    lanes = slice(part * DK, (part + 1) * DK)
    first = TAP_ROW + head * 12 + branch * 4
    total = buffer_ref[base_row : base_row + STEP, lanes] * taps_ref[first + 3 : first + 4, :]
    for behind in range(1, 4):
        moved = buffer_ref[base_row - behind : base_row - behind + STEP, lanes]
        tap = first + 3 - behind
        total = total + keep(reach[behind], moved * taps_ref[tap : tap + 1, :])
    return total


def tn_product(a, b):
    ah, al = hi_lo(a)
    bh, bl = hi_lo(b)
    both = tn(ah, jnp.concatenate([bh, bl], axis=1))
    n = b.shape[1]
    return both[:, :n] + both[:, n:] + tn(al, bh)


def col_sum(x):
    return jnp.sum(x, axis=0, keepdims=True)


def whole(*shape):
    return pl.BlockSpec(shape, lambda *_: (0,) * len(shape))


def sds(shape, kind):
    return jax.ShapeDtypeStruct(shape, kind)


def any_ref():
    return pl.BlockSpec(memory_space=pl.ANY)


def call(kernel, args, after, prefetch, grid, in_specs, out_specs, out_shape, scratch, micros):
    given = len(args)

    def body(*refs):
        return kernel(*refs[:given], *refs[given + len(after) :])

    return pl.pallas_call(
        body,
        grid_spec=pltpu.PrefetchScalarGridSpec(
            num_scalar_prefetch=prefetch, grid=grid, in_specs=list(in_specs) + [any_ref()] * len(after),
            out_specs=out_specs, scratch_shapes=scratch,
        ),
        out_shape=out_shape,
        compiler_params=pltpu.CompilerParams(vmem_limit_bytes=VMEM_LIMIT),
        cost_estimate=pl.CostEstimate(flops=int(micros * 8e8 * COST), bytes_accessed=0, transcendentals=0),
    )(*args, *after)


def shard_copies(own, shards, lanes, target, sems, depth):
    copies = []
    for k, shard in enumerate(shards):
        row = pl.multiple_of((own ^ k) * depth, depth)
        copies.append(pltpu.make_async_copy(shard.at[:, lanes], target.at[pl.ds(row, depth), :], sems.at[k]))
    return copies


def run_copies(copies):
    for copy in copies:
        copy.start()
    for copy in copies:
        copy.wait()


def slot(index, count):
    out = 0
    while count > 1:
        out, index, count = out * 2 + index % 2, index // 2, count // 2
    return out


def feature_rows(shards, depth):
    each = DK // shards
    row = iota((depth * shards, DK), 0)
    col = iota((depth * shards, DK), 1)
    inside = row % depth
    return ((inside < each) & ((row // depth) * each + inside == col)).astype(F32).astype(BF)


def mixer_fwd_kernel(*refs, first_row, shards, depth, width):
    step = pl.program_id(0)
    if shards:
        me_ref, ends_ref, tok_ref = refs[:3]
        shard_refs, refs = refs[3 : 3 + shards], refs[3 + shards :]
        outs, (buffer, state, sems) = refs[:15], refs[15:]
        w_ref, gain_ref, taps_ref, s_out_ref, halo_out_ref = outs[10:]
        outs = outs[:10]
    else:
        me_ref, ends_ref, tok_ref, w_ref, gain_ref, taps_ref, s_in_ref, halo_ref = refs[:8]
        outs, s_out_ref, halo_out_ref, (buffer, state) = refs[8:18], refs[18], refs[19], refs[20:]
    proj_ref, qkv_ref, beta_ref, mixed_ref, normed_ref, inv_ref, wu_ref, r_ref, pm_ref, state_ref = outs
    base = first_row + step * STEP

    @pl.when(step == 0)
    def _():
        if shards:
            copies = shard_copies(me_ref[0], shard_refs, slice(0, 896), w_ref, sems.at[0], depth)
            copies += shard_copies(me_ref[0], shard_refs, slice(896, 1152), normed_ref, sems.at[1], depth)
            run_copies(copies)
            extra = w_ref[:, 768:896]
            pick = (iota((8, DK), 1) == iota((8, DK), 0) + 2).astype(F32).astype(BF)
            gain_ref[...] = nt(pick, extra)
            taps_ref[...] = tn(extra, feature_rows(shards, depth))[:32]
            state[...] = jnp.zeros_like(state)
            buffer[0:8, :] = jnp.zeros((8, 768), F32)
        else:
            state[...] = s_in_ref[...]
            buffer[0:8, :] = halo_ref[...]

    tok = tok_ref[...].astype(F32)
    scale = lax.rsqrt(jnp.mean(tok * tok, axis=-1, keepdims=True) + EPS)
    low_in = (tok * scale * gain_ref[0:1, :]).astype(BF)
    proj = nn(low_in, w_ref[...])
    buffer[8 : 8 + STEP, :] = proj[:, :768]
    proj_ref[...] = proj[:, :768]
    betas = sigmoid(proj[:, 768:896])
    beta_ref[...] = betas
    beta_t = betas.T
    rows, same, carry, in_last, go_on = doc_masks(ends_ref, base)
    behind = base + iota((STEP, DK), 0) - rows
    reach = [None] + [behind >= s for s in (1, 2, 3)]
    parts = []
    for part in range(6):
        pre = conv_of(buffer, taps_ref, part, reach, 8)
        act = pre * sigmoid(pre)
        if part < 4:
            norm = lax.rsqrt(jnp.sum(act * act, axis=-1, keepdims=True) + EPS)
            act = act * norm
            if part < 2:
                act = act * DK**-0.5
        parts.append(act.astype(BF))
    halo_out_ref[...] = buffer[STEP : STEP + 8, :]
    buffer[0:8, :] = buffer[STEP : STEP + 8, :]
    qkv_ref[...] = jnp.concatenate(parts, axis=1)
    at_row = iota((STEP, STEP), 0)
    at_col = iota((STEP, STEP), 1)
    strict = same & (at_row > at_col)
    lower = same & (at_row >= at_col)
    heads = range(2)
    q, k, v = parts[0:2], parts[2:4], parts[4:6]
    lows = [keep(strict, nt(k[h], k[h]) * betas[:, h : h + 1]) for h in heads]
    invs = inverses(lows)
    head_gain = taps_ref[HEAD_ROW : HEAD_ROW + 1, :]
    for h in heads:
        inv_ref[0, h] = invs[h].astype(BF)
        scaled_h, scaled_l = hi_lo(invs[h] * beta_t[h : h + 1, :])
        kv = jnp.concatenate([k[h], v[h]], axis=1)
        solved = nn(scaled_h, kv) + nn(scaled_l, kv)
        wu_ref[0, h] = solved.astype(BF)
        w = keep(carry, solved[:, :DK])
        both_h, both_l = hi_lo(jnp.concatenate([solved[:, DK:], w], axis=1))
        scores = keep(lower, nt(q[h], k[h])).astype(BF)
        inside = nn(scores, both_h)
        k_last = keep(in_last, k[h].astype(F32)).astype(BF)
        outer = tn(k_last, both_h) + tn(k_last, both_l)
        r = (keep(carry, q[h].astype(F32)) - inside[:, DK:]).astype(BF)
        r_ref[0, h] = r
        pm_ref[0, h] = outer[:, DK:]
        now = state[h]
        now_h, now_l = hi_lo(now)
        state_ref[0, h] = now_h
        out = nn(r, jnp.concatenate([now_h, now_l], axis=1))
        mixed = inside[:, :DK] + out[:, :DK] + out[:, DK:]
        state[h] = go_on * now - product(outer[:, DK:], now) + outer[:, :DK]
        lanes = slice(h * DK, (h + 1) * DK)
        mixed_ref[:, lanes] = mixed
        scale = lax.rsqrt(jnp.mean(mixed * mixed, axis=-1, keepdims=True) + EPS)
        head_normed = (mixed * scale * head_gain).astype(BF)
        if shards:
            normed_ref[pl.ds(pl.multiple_of(width + step * STEP, STEP), STEP), lanes] = head_normed
        else:
            normed_ref[:, lanes] = head_normed
    s_out_ref[...] = state[...]


def mixer_fwd(me, ends, tokens, count, first_row, after=(), shards=None, w_in=None, small=None, carried=None):
    width = tokens.shape[1]
    steps = count // STEP
    start = first_row // STEP
    rows = lambda n, at=0: pl.BlockSpec((STEP, n), lambda i: (i + at, 0))
    group = lambda *s: pl.BlockSpec((1,) + s, lambda i: (i,) + (0,) * len(s))
    smem = pl.BlockSpec(memory_space=pltpu.SMEM)
    out_specs = [
        rows(768), rows(768), rows(DK), rows(256), rows(256),
        group(2, STEP, STEP), group(2, STEP, STEP), group(2, STEP, DK), group(2, DK, DK), group(2, DK, DK),
    ]
    out_shape = [
        sds((count, 768), F32), sds((count, 768), BF), sds((count, DK), F32), sds((count, 256), F32),
        sds((count, 256), BF), sds((steps, 2, STEP, STEP), BF), sds((steps, 2, STEP, STEP), BF),
        sds((steps, 2, STEP, DK), BF), sds((steps, 2, DK, DK), F32), sds((steps, 2, DK, DK), BF),
    ]
    scratch = [pltpu.VMEM((STEP + 8, 768), F32), pltpu.VMEM((2, DK, DK), F32)]
    if shards:
        args = [me, ends, tokens, *shards]
        in_specs = [smem, smem, rows(width, start)] + [any_ref()] * len(shards)
        out_specs[4] = whole(width + count, 256)
        out_shape[4] = sds((width + count, 256), BF)
        out_specs += [whole(width, 896), whole(8, width), whole(32, DK)]
        out_shape += [sds((width, 896), BF), sds((8, width), F32), sds((32, DK), F32)]
        scratch.append(pltpu.SemaphoreType.DMA((2, len(shards))))
    else:
        args = [me, ends, tokens, w_in, *small, *carried]
        in_specs = [
            smem, smem, rows(width, start), whole(width, 896), whole(8, width), whole(32, DK),
            whole(2, DK, DK), whole(8, 768),
        ]
    out_specs += [whole(2, DK, DK), whole(8, 768)]
    out_shape += [sds((2, DK, DK), F32), sds((8, 768), F32)]
    return call(
        functools.partial(
            mixer_fwd_kernel, first_row=first_row, shards=len(shards) if shards else 0,
            depth=shards[0].shape[0] if shards else 0, width=width,
        ),
        args, after, 0, (steps,), in_specs, out_specs, out_shape, scratch, 6 * steps,
    )


def mixer_bwd_kernel(*refs, first_row, steps, first, last, shards, depth):
    step = pl.program_id(0)
    (
        me_ref, ends_ref, mine_ref, theirs_ref, res_ref, cot_ref, tok_ref, proj_ref, prev_ref, before_ref, qkv_ref, beta_ref, mixed_ref, normed_ref,
        inv_ref, wu_ref, r_ref, pm_ref, state_ref, w_ref, wo_ref, gain_ref, taps_ref,
    ) = refs[:23]
    refs = refs[23:]
    if not first:
        gw_in, gwo_in, gsmall_in, gnorm_in, ds_in_ref, halo_ref = refs[:6]
        refs = refs[6:]
    if last:
        ggain_refs, refs = refs[:2], refs[2:]
    dn_mine, dn_theirs, d_att_ref = refs[:3]
    refs = refs[3:]
    if last:
        same_ref, other_ref, refs = refs[0], refs[1], refs[2:]
    else:
        out_refs, refs = refs[:6], refs[6:]
    buffer, ahead, dstate, back_s, gw_ref, gwo_ref, gsmall_ref, gnorm_ref = refs
    tile = steps - 1 - step
    base = first_row + tile * STEP
    half = tile // (steps // 2)
    core = me_ref[1] & 1

    @pl.when(step == 0)
    def _():
        if first:
            dstate[...] = jnp.zeros_like(dstate)
            ahead[:, 0:8, :] = jnp.zeros((3, 8, 768), F32)
            gw_ref[...] = jnp.zeros_like(gw_ref)
            gwo_ref[...] = jnp.zeros_like(gwo_ref)
            gsmall_ref[...] = jnp.zeros_like(gsmall_ref)
            gnorm_ref[...] = jnp.zeros_like(gnorm_ref)
        else:
            dstate[...] = ds_in_ref[...]
            ahead[:, 0:8, :] = halo_ref[...]
            gw_ref[...] = gw_in[...]
            gwo_ref[...] = gwo_in[...]
            gsmall_ref[...] = gsmall_in[...]
            gnorm_ref[...] = gnorm_in[...]

    @pl.when(half == core)
    def _():
        back_s[...] = mine_ref[...]

    @pl.when(half != core)
    def _():
        back_s[...] = theirs_ref[...]

    ahead[:, STEP : STEP + 8, :] = ahead[:, 0:8, :]
    d_resid = cot_ref[...].astype(F32) + norm_back(back_s[...].astype(F32), res_ref[...], gain_ref[1:2, :])
    d_att = d_resid.astype(BF)
    d_att_ref[...] = d_att
    d_head = nn(d_att, wo_ref[...])
    gwo_ref[...] += tn(d_att, normed_ref[...])
    rows, same, carry, in_last, go_on = doc_masks(ends_ref, base)
    at_row = iota((STEP, STEP), 0)
    at_col = iota((STEP, STEP), 1)
    strict = same & (at_row > at_col)
    lower = same & (at_row >= at_col)
    strict_t = same & (at_row < at_col)
    lower_t = same & (at_row <= at_col)
    betas = beta_ref[...]
    beta_t = betas.T
    heads = range(2)
    d_mixer = [None] * 6
    lane = iota((STEP, DK), 1)
    d_beta = jnp.zeros((STEP, DK), F32)
    head_gain = taps_ref[HEAD_ROW : HEAD_ROW + 1, :]
    for h in heads:
        lanes = slice(h * DK, (h + 1) * DK)
        mixed = mixed_ref[:, lanes]
        e = d_head[:, lanes]
        scale = lax.rsqrt(jnp.mean(mixed * mixed, axis=-1, keepdims=True) + EPS)
        unit = mixed * scale
        gsmall_ref[HEAD_ROW : HEAD_ROW + 1, :] += col_sum(e * unit)
        ge = e * head_gain
        d_out = (scale * (ge - unit * jnp.mean(unit * ge, axis=-1, keepdims=True))).astype(BF)
        q = qkv_ref[:, h * DK : (h + 1) * DK]
        k = qkv_ref[:, 256 + h * DK : 256 + (h + 1) * DK]
        v = qkv_ref[:, 512 + h * DK : 512 + (h + 1) * DK]
        wu = wu_ref[0, h]
        inv = inv_ref[0, h]
        r = r_ref[0, h]
        s_in = state_ref[0, h]
        beta_col = betas[:, h : h + 1]
        beta_row = beta_t[h : h + 1, :]
        dst = dstate[h]
        ds_h = dst.astype(BF)
        dstate[h] = go_on * dst - tn_product(pm_ref[0, h], dst) + tn(r, d_out)
        scores_t = keep(lower_t, nt(k, q)).astype(BF)
        k_last = keep(in_last, k.astype(F32)).astype(BF)
        d_x = nn(scores_t, d_out) + nn(k_last, ds_h)
        carried_w = keep(carry, wu[:, :DK].astype(F32)).astype(BF)
        x = (wu[:, DK:].astype(F32) - nn(carried_w, s_in)).astype(BF)
        d_xb = d_x.astype(BF)
        d_scores = keep(lower, nt(d_out, x)).astype(BF)
        d_scores_t = keep(lower_t, nt(x, d_out)).astype(BF)
        back_s = nt(jnp.concatenate([d_out, d_xb], axis=0), s_in)
        d_q = keep(carry, back_s[:STEP]) + nn(d_scores, k)
        d_k = nn(d_scores_t, q) + keep(in_last, nt(x, ds_h))
        d_w = -keep(carry, back_s[STEP:])
        z = tn(inv, jnp.concatenate([d_w.astype(BF), d_xb], axis=1))
        z_b = z.astype(BF)
        d_a = -keep(strict, nt(z_b, wu))
        d_a_t = -keep(strict_t, nt(wu, z_b))
        gram = nt(k, k)
        kv = jnp.concatenate([k, v], axis=1).astype(F32)
        d_b = jnp.sum(d_a * gram + z * kv, axis=-1, keepdims=True)
        d_g = (d_a * beta_col + d_a_t * beta_row).astype(BF)
        d_k = d_k + nn(d_g, k) + beta_col * z[:, :DK]
        d_v = beta_col * z[:, DK:]
        for place, grad in ((h, d_q), (2 + h, d_k), (4 + h, d_v)):
            d_mixer[place] = grad.astype(BF).astype(F32)
        d_beta = jnp.where(lane == h, d_b * beta_col * (1.0 - beta_col), d_beta)
    before = before_ref[...] if first_row else jnp.zeros((8, 768), F32)
    buffer[0:8, :] = jnp.where(tile == 0, before, prev_ref[...])
    buffer[8 : 8 + STEP, :] = proj_ref[...]
    behind = base + iota((STEP, DK), 0) - rows
    reach = [None] + [behind >= s for s in (1, 2, 3)]
    d_proj = []
    for part in range(6):
        branch, head = divmod(part, 2)
        lanes = slice(part * DK, (part + 1) * DK)
        tap0 = TAP_ROW + head * 12 + branch * 4
        pre = conv_of(buffer, taps_ref, part, reach, 8)
        sig = sigmoid(pre)
        act = pre * sig
        grad = d_mixer[part]
        if part < 4:
            norm = lax.rsqrt(jnp.sum(act * act, axis=-1, keepdims=True) + EPS)
            unit = act * norm
            grad = norm * (grad - unit * jnp.sum(unit * grad, axis=-1, keepdims=True))
            if part < 2:
                grad = grad * DK**-0.5
        grad = grad * sig * (1.0 + pre * (1.0 - sig))
        d_in = grad * taps_ref[tap0 + 3 : tap0 + 4, :]
        gsmall_ref[tap0 + 3 : tap0 + 4, :] += col_sum(grad * buffer[8 : 8 + STEP, lanes])
        for s in (1, 2, 3):
            tap = tap0 + 3 - s
            masked = keep(reach[s], grad)
            gsmall_ref[tap : tap + 1, :] += col_sum(masked * buffer[8 - s : 8 - s + STEP, lanes])
            ahead[s - 1, 0:STEP, lanes] = masked
            d_in = d_in + ahead[s - 1, s : s + STEP, lanes] * taps_ref[tap : tap + 1, :]
        d_proj.append(d_in.astype(BF))
    d_proj.append(d_beta.astype(BF))
    d_proj = jnp.concatenate(d_proj, axis=1)
    tok = tok_ref[...].astype(F32)
    unit = tok * lax.rsqrt(jnp.mean(tok * tok, axis=-1, keepdims=True) + EPS)
    low_in = (unit * gain_ref[0:1, :]).astype(BF)
    gw_ref[...] += tn(low_in, d_proj)
    d_normed = nt(d_proj, w_ref[...])
    gnorm_ref[0:1, :] += col_sum(d_normed * unit)

    @pl.when(half == core)
    def _():
        dn_mine[...] = d_normed.astype(BF)

    @pl.when(half != core)
    def _():
        dn_theirs[...] = d_normed.astype(BF)

    @pl.when(step == steps - 1)
    def _():
        if last:
            small = jnp.concatenate([gsmall_ref[...], jnp.zeros((DK - 32, DK), F32)], axis=0).astype(BF)
            gnorm_ref[1:2, :] = ggain_refs[0][0:1, :] + ggain_refs[1][0:1, :]
            spot = (iota((8, DK), 1) == 2 + iota((8, DK), 0)) & (iota((8, DK), 0) < 2)
            extra = tn(gnorm_ref[...].astype(BF), spot.astype(F32).astype(BF))
            gw_ref[:, 768:896] += nt(feature_rows(shards, depth), small) + extra
            for k in range(shards):
                row = pl.multiple_of((me_ref[0] ^ k) * depth, depth)
                target = same_ref if k % 2 == 0 else other_ref
                place = slot(k // 2, shards // 2)
                target[place, :, 0:896] = gw_ref[pl.ds(row, depth), :].astype(BF)
                target[place, :, 896:1152] = gwo_ref[pl.ds(row, depth), :].astype(BF)
        else:
            for out, value in zip(out_refs, (gw_ref, gwo_ref, gsmall_ref, gnorm_ref, dstate)):
                out[...] = value[...]
            out_refs[5][...] = ahead[:, 0:8, :]


def mixer_bwd(me, ends, mine, theirs, res, cot, tokens, saved, w_in, wo_own, small, first_row, carried, last, shards, after=(), ggain=None):
    proj, qkv, betas, mixed, normed, inv, wu, r, pm, states, prev, normed_at = saved
    count, width = proj.shape[0], tokens.shape[1]
    steps = count // STEP
    per_half = steps // 2
    start = first_row // STEP
    rows = lambda n, at=0: pl.BlockSpec((STEP, n), lambda i, me: (steps - 1 - i + at, 0))
    group = lambda *s: pl.BlockSpec((1,) + s, lambda i, me: (steps - 1 - i,) + (0,) * len(s))

    def half_rows(flip):
        def place(i, me):
            tile = steps - 1 - i
            half, inside = tile // per_half, tile % per_half
            wanted = (me[1] & 1) ^ flip
            return (jnp.where(half == wanted, inside, jnp.where(half > wanted, per_half - 1, 0)), 0)

        return pl.BlockSpec((STEP, width), place)

    in_specs = [
        pl.BlockSpec(memory_space=pltpu.SMEM), half_rows(0), half_rows(1), rows(width), rows(width, start), rows(width, start), rows(768),
        pl.BlockSpec((8, 768), lambda i, me: (jnp.maximum((steps - 1 - i) * (STEP // 8) - 1, 0), 0)),
        whole(8, 768), rows(768), rows(DK), rows(256), rows(256, normed_at),
        group(2, STEP, STEP), group(2, STEP, STEP), group(2, STEP, DK), group(2, DK, DK), group(2, DK, DK),
        whole(width, 896), whole(width, 256), whole(8, width), whole(32, DK),
    ]
    args = [
        me, ends, mine, theirs, res, cot, tokens, proj, proj, prev, qkv, betas, mixed, normed, inv, wu, r, pm, states, w_in, wo_own,
        *small,
    ]
    sums = [(width, 896), (width, 256), (32, DK), (8, width), (2, DK, DK), (3, 8, 768)]
    if carried is not None:
        args += carried
        in_specs += [whole(*s) for s in sums]
    if last:
        args += ggain
        in_specs += [whole(8, width)] * 2
    depth = width // shards
    out_specs = [half_rows(0), half_rows(1), rows(width)]
    out_shape = [sds((count // 2, width), BF)] * 2 + [sds((count, width), BF)]
    if last:
        out_specs += [whole(shards // 2, depth, 1152)] * 2
        out_shape += [sds((shards // 2, depth, 1152), BF)] * 2
    else:
        out_specs += [whole(*s) for s in sums]
        out_shape += [sds(s, F32) for s in sums]
    return call(
        functools.partial(
            mixer_bwd_kernel, first_row=first_row, steps=steps, first=carried is None, last=last, shards=shards,
            depth=depth,
        ),
        args, after, 1, (steps,), in_specs, out_specs, out_shape,
        [
            pltpu.VMEM((STEP + 8, 768), F32), pltpu.VMEM((3, STEP + 8, 768), F32), pltpu.VMEM((2, DK, DK), F32),
            pltpu.VMEM((STEP, width), BF), pltpu.VMEM((width, 896), F32), pltpu.VMEM((width, 256), F32),
            pltpu.VMEM((32, DK), F32), pltpu.VMEM((8, width), F32),
        ],
        7 * steps,
    )


def mlp_kernel(*refs, steps, shards, depth, ff):
    step = pl.program_id(0)
    me_ref, tok_ref, cot_ref, gain_ref = refs[:4]
    head_refs, refs = refs[4:8], refs[8:]
    if shards:
        shard_refs, wo_refs, refs = refs[:shards], refs[shards : shards + 4], refs[shards + 4 :]
    else:
        g_ref, u_ref, d_ref, wo_ref = refs[:4]
        refs = refs[4:]
    back_mine, back_theirs, down_mine, down_theirs, res_ref, normed_ref, act_ref, dg_ref, du_ref, ggain_ref = refs[:10]
    refs = refs[10:]
    if shards:
        g_ref, u_ref, d_ref, wo_ref, heads, raw, sems, wo_sems = refs
    else:
        (heads,) = refs
    own = me_ref[1]

    @pl.when(step == 0)
    def _():
        ggain_ref[...] = jnp.zeros_like(ggain_ref)
        if shards:
            copies = shard_copies(me_ref[0], shard_refs, slice(None), raw, sems, depth)
            width = raw.shape[0]
            copies += [pltpu.make_async_copy(wo_refs[m].at[pl.ds(0, width), :], wo_ref.at[own ^ m], wo_sems.at[m]) for m in range(4)]
            run_copies(copies)
            inside = iota((256, FF_PAD), 1) < ff
            for at in range(0, raw.shape[0], 256):
                here = slice(at, at + 256)
                g_ref[here, :] = keep(inside, raw[here, 0:FF_PAD].astype(F32)).astype(BF)
                from_u = ff - ff % 128
                turned = pltpu.roll(
                    raw[here, from_u : from_u + FF_PAD].astype(F32), FF_PAD - ff % 128, axis=1
                )
                u_ref[here, :] = keep(inside, turned).astype(BF)
                from_d = 2 * ff
                d_ref[here, :] = keep(inside, raw[here, from_d : from_d + FF_PAD].astype(F32)).astype(BF)

    for m in range(4):
        heads[own ^ m] = head_refs[m][...]
    attended = nt(heads[0], wo_ref[0])
    for m in range(1, 4):
        attended = attended + nt(heads[m], wo_ref[m])
    res = tok_ref[...].astype(F32) + attended
    res_ref[...] = res
    unit = res * lax.rsqrt(jnp.mean(res * res, axis=-1, keepdims=True) + EPS)
    normed = (unit * gain_ref[1:2, :]).astype(BF)
    normed_ref[...] = normed
    gate = nn(normed, g_ref[...])
    up = nn(normed, u_ref[...])
    sig = sigmoid(gate)
    silu = gate * sig
    act = (silu * up).astype(BF)
    act_ref[...] = act
    d_hidden = nn(cot_ref[...], d_ref[...])
    d_gate = (d_hidden * up * sig * (1.0 + gate * (1.0 - sig))).astype(BF)
    d_up = (d_hidden * silu).astype(BF)
    dg_ref[...] = d_gate
    du_ref[...] = d_up
    down = nt(act, d_ref[...]).astype(BF)
    back = nt(d_gate, g_ref[...]) + nt(d_up, u_ref[...])
    ggain_ref[0:1, :] += col_sum(back * unit)

    @pl.when(step < steps // 2)
    def _():
        back_theirs[...] = back.astype(BF)
        down_theirs[...] = down

    @pl.when(step >= steps // 2)
    def _():
        back_mine[...] = back.astype(BF)
        down_mine[...] = down


def mlp(me, tokens, cot, small, heads, heads_at, count, first_row, ff, after=(), shards=None, wo=None, weights=None):
    width = tokens.shape[1]
    steps = count // STEP
    per_half = steps // 2
    start = first_row // STEP

    def tile(i, me, at=0):
        half = jnp.where(i >= per_half, me[1] & 1, 1 - (me[1] & 1))
        return at + half * per_half + i % per_half

    rows = lambda n, at=0: pl.BlockSpec((STEP, n), lambda i, me: (tile(i, me, at), 0))
    theirs = pl.BlockSpec((STEP, width), lambda i, me: (jnp.minimum(i, per_half - 1), 0))
    mine = pl.BlockSpec((STEP, width), lambda i, me: (jnp.maximum(i - per_half, 0), 0))
    in_specs = [rows(width, start), rows(width, start), whole(8, width)] + [rows(256, heads_at)] * 4
    args = [me, tokens, cot, small[0], *heads]
    out_specs = [mine, theirs, mine, theirs, rows(width), rows(width), rows(FF_PAD), rows(FF_PAD), rows(FF_PAD), whole(8, width)]
    halves = (count // 2, width)
    out_shape = [
        sds(halves, BF), sds(halves, BF), sds(halves, BF), sds(halves, BF), sds((count, width), F32), sds((count, width), BF),
        sds((count, FF_PAD), BF), sds((count, FF_PAD), BF), sds((count, FF_PAD), BF), sds((8, width), F32),
    ]
    kept = [(width, FF_PAD)] * 3 + [(4, width, 256)]
    scratch = [pltpu.VMEM((4, STEP, 256), BF)]
    if shards:
        in_specs += [any_ref()] * (len(shards) + 4)
        args += [*shards, *wo]
        out_specs += [whole(*s) for s in kept]
        out_shape += [sds(s, BF) for s in kept]
        scratch += [
            pltpu.VMEM((width, shards[0].shape[1]), BF),
            pltpu.SemaphoreType.DMA((len(shards),)), pltpu.SemaphoreType.DMA((4,)),
        ]
    else:
        in_specs += [whole(*s) for s in kept]
        args += weights
    return call(
        functools.partial(
            mlp_kernel, steps=steps, shards=len(shards) if shards else 0, depth=shards[0].shape[0] if shards else 0,
            ff=ff,
        ),
        args, after, 1, (steps,), in_specs, out_specs, out_shape, scratch, 6 * steps,
    )


def mlp_grads_kernel(me_ref, *refs, chunks, shards, depth, ff):
    step = pl.program_id(0)
    left, refs = refs[:chunks], refs[chunks:]
    rights, (same, other, packed) = refs[:-3], refs[-3:]
    each = 256 // depth

    def over_rows(right):
        total = tn(left[0][...], right[0][...])
        for a, b in zip(left[1:], right[1:]):
            total = total + tn(a[...], b[...])
        return total

    first = over_rows(rights[:chunks])
    if len(rights) == chunks:
        packed[...] = first
    else:
        cut = ff - ff % 128
        turned = pltpu.roll(over_rows(rights[chunks:]), ff % 128, axis=1)
        packed[:, 0:cut] = first[:, 0:cut]
        packed[:, cut : cut + 128] = first[:, cut : cut + 128] + turned[:, 0:128]
        packed[:, cut + 128 : 2 * ff] = turned[:, 128 : 2 * ff - cut]
    for i in range(shards // each):

        @pl.when(step == i)
        def _(i=i):
            for t in range(each):
                row = pl.multiple_of((t ^ (me_ref[0] % each)) * depth, depth)
                k = i * each + t
                (same if k % 2 == 0 else other)[slot(k // 2, shards // 2)] = packed[pl.ds(row, depth), :].astype(BF)


def mlp_grads(me, left, left_at, rights, shards, ff, after=()):
    chunks = len(left)
    count, width = rights[0].shape[0], left[0].shape[1]
    depth = width // shards
    each = 256 // depth
    column = lambda at: pl.BlockSpec((count, 256), lambda i, me: (at, (me[0] // each) ^ i))
    wide = FF_PAD if len(rights) == chunks else 2 * ff
    stack = (shards // 2, depth, wide)
    return call(
        functools.partial(mlp_grads_kernel, chunks=chunks, shards=shards, depth=depth, ff=ff),
        (me, *left, *rights), after, 1, (width // 256,),
        [column(at) for at in left_at] + [whole(count, FF_PAD)] * len(rights),
        [whole(*stack)] * 2, [sds(stack, BF)] * 2, [pltpu.VMEM((256, wide), F32)], 6,
    )


def norm_back(e, v, gain):
    scale = lax.rsqrt(jnp.mean(v * v, axis=-1, keepdims=True) + EPS)
    unit = v * scale
    ge = e * gain
    return scale * (ge - unit * jnp.mean(unit * ge, axis=-1, keepdims=True))


def pair_kernel(own_ref, other_ref, out_ref):
    out_ref[...] = own_ref[...] + other_ref[...]


def pair_after(own, other, after):
    vmem = pl.BlockSpec(memory_space=pltpu.VMEM)
    return call(pair_kernel, (own, other), after, 0, (), [vmem] * 2, vmem, sds(own.shape, BF), [], 2)


def split_pair_kernel(own_ref, other_ref, *out_refs):
    rows = out_refs[0].shape[0]
    for i, out_ref in enumerate(out_refs):
        here = slice(i * rows, (i + 1) * rows)
        out_ref[...] = own_ref[here, :] + other_ref[here, :]


def split_pair_after(own, other, after):
    vmem = pl.BlockSpec(memory_space=pltpu.VMEM)
    part = sds((own.shape[0] // 2, own.shape[1]), BF)
    return call(split_pair_kernel, (own, other), after, 0, (), [vmem] * 2, [vmem] * 2, [part] * 2, [], 2)


def gate(x, after):
    return pl.pallas_call(
        lambda *refs: None,
        in_specs=[any_ref()] * (1 + len(after)),
        out_specs=any_ref(),
        out_shape=sds(x.shape, x.dtype),
        input_output_aliases={0: 0},
        cost_estimate=pl.CostEstimate(flops=0, bytes_accessed=0, transcendentals=0),
    )(x, *after)


def final_kernel(me_ref, mine_ref, theirs_ref, base_ref, tok_ref, gain_ref, *refs):
    out_ref, moved = refs[-2:]
    first = pl.program_id(0) < pl.num_programs(0) // 2
    low_core = (me_ref[1] & 1) == 0

    @pl.when(first == low_core)
    def _():
        moved[...] = mine_ref[...]

    @pl.when(first != low_core)
    def _():
        moved[...] = theirs_ref[...]

    part = moved[...].astype(F32)
    if out_ref.dtype == F32:
        part = norm_back(part, tok_ref[...].astype(F32), gain_ref[0:1, :])
    out_ref[...] = (base_ref[...].astype(F32) + part).astype(out_ref.dtype)


def final(me, mine, theirs, base, tokens, gain, first_row, kind, into=None):
    count, width = base.shape
    size = TILE
    tiles = count // 2 // size
    start = first_row // size

    def half_rows(flip):
        def place(i, me):
            half, inside = i // tiles, i % tiles
            wanted = (me[1] & 1) ^ flip
            return (jnp.where(half == wanted, inside, jnp.where(half > wanted, tiles - 1, 0)), 0)

        return pl.BlockSpec((size, width), place)

    rows = lambda at: pl.BlockSpec((size, width), lambda i, me: (at + i, 0))
    args = [me, mine, theirs, base, tokens, gain]
    in_specs = [half_rows(0), half_rows(1), rows(0), rows(start) if kind == F32 else rows(start), whole(8, width)]
    if into is not None:
        args.append(into)
        in_specs.append(any_ref())
    return pl.pallas_call(
        final_kernel,
        grid_spec=pltpu.PrefetchScalarGridSpec(
            num_scalar_prefetch=1, grid=(2 * tiles,), in_specs=in_specs, out_specs=rows(start),
            scratch_shapes=[pltpu.VMEM((size, width), BF)],
        ),
        out_shape=sds(tokens.shape, kind),
        input_output_aliases={6: 0} if into is not None else {},
        compiler_params=pltpu.CompilerParams(vmem_limit_bytes=VMEM_LIMIT),
        cost_estimate=pl.CostEstimate(flops=int(1e9 * COST), bytes_accessed=0, transcendentals=0),
    )(*args)


def swap(x, axis, k):
    return lax.ppermute(x, axis, [(i, i ^ k) for i in range(lax.axis_size(axis))])


def pair_sum(own, other):
    return own + other


def finish(same, other, bit, after=()):
    sent = other
    while same.shape[0] > 1:
        half = same.shape[0] // 2
        same, sent = same[:half] + other[:half], same[half:] + other[half:]
        bit *= 2
        other = swap(sent, "dp", bit)
        if after:
            other, after = gate(other, after), ()
    return same, other, sent


def last_sum(same, other):
    return same[0].astype(F32) + other[0].astype(F32)


def on_device(
    tokens, doc_lengths, cotangent, norm_gain, w_query, w_key, w_value, w_beta, conv_taps, head_gain, w_out, mlp_gain,
    w_gate, w_up, w_down,
):
    seq_rows, length, width = tokens.shape
    shards = lax.axis_size("dp")
    depth = width // shards
    each = conv_taps.shape[2]
    ff = w_gate.shape[1]
    me = jnp.stack([lax.axis_index("dp"), lax.axis_index("mp")]).astype(jnp.int32)
    ends = jnp.cumsum(doc_lengths[0]).astype(jnp.int32)
    flat = tokens.reshape(length, width)
    cot = cotangent.reshape(length, width)
    tall = lambda x: jnp.pad(x, ((0, depth - x.shape[0]), (0, 0)))
    pack = jnp.concatenate(
        [
            w_query, w_key, w_value, w_beta, norm_gain[:, None], mlp_gain[:, None],
            tall(conv_taps.reshape(24, each).T), tall(head_gain[:, None]), jnp.zeros((depth, 99), BF), w_out.T,
        ],
        axis=1,
    )
    total = length
    count = length // CHUNKS
    far = [swap(pack, "dp", k) for k in range(2, shards, 2)]
    near = [swap(x, "dp", 1) for x in [pack] + far]
    mixer_shards = [x for pair in zip([pack] + far, near) for x in pair]
    def second_pack(filler):
        return jnp.concatenate([w_gate, w_up, w_down.T, filler[:depth, : FF_PAD - ff]], axis=1)

    pack_two = second_pack(far[-1])
    steps_two = list(range(2, shards, 2))
    far_two = [swap(pack_two, "dp", k) for k in steps_two[:-1]]
    one, two = ORDER
    near_two = [swap(pack_two, "dp", 1)]
    out = mixer_fwd(me, ends, flat, count, 0, shards=mixer_shards)
    fwd = [list(out[:10]) + [out[14], width // STEP]]
    w_in, small = out[10], (out[11], out[12])
    pack_late = second_pack(out[4])
    head_far = swap(out[4], "mp", 2)
    head_near = swap(out[4], "mp", 1)
    near_two += [swap(x, "dp", 1) for x in far_two]
    far_two.append(swap(pack_late, "dp", steps_two[-1]))
    carried = out[13:]
    out = mixer_fwd(
        me, ends, flat, count, count, after=far_two[:-1] + near_two[:1], w_in=w_in, small=small, carried=carried
    )
    fwd.append(list(out[:10]) + [carried[1], 0])
    own = gate(out[4], [head_far, head_near, far_two[-1]] + near_two[1:])
    fwd[1][4] = own
    near_two.append(swap(far_two[-1], "dp", 1))
    mlp_shards = [x for pair in zip([pack_two] + far_two, near_two) for x in pair]
    far_heads = swap(own, "mp", 2)
    heads = [
        [fwd[0][4], head_near, head_far, swap(head_far, "mp", 1)],
        [own, swap(own, "mp", 1), far_heads, swap(far_heads, "mp", 1)],
    ]
    wo_own = fwd[0][4]
    mid = {}
    out = mlp(
        me, flat, cot, small, heads[one], fwd[one][11], count, one * count, ff, shards=mlp_shards, wo=heads[0],
        after=heads[two][1:],
    )
    weights, mid[one] = list(out[10:]), out[:10]
    p_one = pair_sum(out[0], swap(out[1], "mp", 1))
    q_one = swap(p_one, "mp", 2)
    down_one = swap(out[3], "mp", 1)
    out = mlp(me, flat, cot, small, heads[two], fwd[two][11], count, two * count, ff, after=[p_one], weights=weights)
    mid[two] = out
    p_two = pair_sum(out[0], swap(gate(out[1], [q_one, down_one]), "mp", 1))
    q_two = swap(p_two, "mp", 2)
    down_two = swap(out[3], "mp", 1)
    s_one = p_one + q_one
    s_one_other = swap(s_one, "mp", 1)
    chunks = (one, two)
    same_a, other_a = mlp_grads(
        me, [mid[c][5] for c in chunks], [0] * CHUNKS, [mid[c][7] for c in chunks] + [mid[c][8] for c in chunks],
        shards, ff, after=[p_two, s_one],
    )
    same_b, other_b = mlp_grads(
        me, [cot] * CHUNKS, chunks, [mid[c][6] for c in chunks], shards, ff, after=[same_a],
    )
    s_two = pair_after(p_two, q_two, [same_b, s_one_other, down_one, down_two])
    s_two_other = swap(s_two, "mp", 1)
    down_one = pair_after(mid[one][2], down_one, [s_two])
    far_one = swap(down_one, "mp", 2)
    down_parts = split_pair_after(mid[two][2], down_two, [down_one])
    far_part = swap(down_parts[0], "mp", 2)
    other_a = swap(other_a, "dp", 1)
    other_b = swap(other_b, "dp", 1)
    out_one = mixer_bwd(
        me, ends, s_one, s_one_other, mid[one][4], cot, flat, fwd[one], w_in, wo_own, small, one * count, None, False,
        shards, after=[down_parts[0]],
    )
    other_a, other_b = gate(other_a, [out_one[0]]), gate(other_b, [out_one[0]])
    n_one = pair_sum(out_one[0], swap(gate(out_one[1], [far_one, far_part, other_a, other_b, s_two_other]), "mp", 1))
    m_one = swap(n_one, "mp", 2)
    far_parts = [far_part, swap(gate(down_parts[1], [n_one]), "mp", 2)]
    half = shards // 4
    same_a, other_a = same_a[:half] + other_a[:half], same_a[half:] + other_a[half:]
    other_a = swap(other_a, "dp", 2)
    same_b, other_b = same_b[:half] + other_b[:half], same_b[half:] + other_b[half:]
    other_b = swap(other_b, "dp", 2)
    out_two = mixer_bwd(
        me, ends, s_two, s_two_other, mid[two][4], cot, flat, fwd[two], w_in, wo_own, small, two * count,
        list(out_one[3:]), True, shards, after=[n_one, same_a, same_b], ggain=(mid[one][9], mid[two][9]),
    )
    other_mix = swap(out_two[4], "dp", 1)
    n_theirs = gate(out_two[1], [m_one, far_parts[1], other_a, other_b])
    sum_a, sum_b = finish(same_a, other_a, 2), finish(same_b, other_b, 2)
    n_two = pair_after(out_two[0], swap(n_theirs, "mp", 1), [sum_a[2], sum_b[2]])
    m_two = swap(n_two, "mp", 2)
    layer_out = token_grad = None
    sent = jnp.concatenate([d + f for d, f in zip(down_parts, far_parts)], axis=0)
    for c, sent in ((one, down_one + far_one), (two, sent)):
        layer_out = final(me, sent, swap(sent, "mp", 1), mid[c][4], flat, small[0], c * count, BF, layer_out)
    sent = n_one + m_one
    token_grad = final(me, sent, swap(sent, "mp", 1), out_one[2], flat, small[0], one * count, F32, None)
    other_mix = gate(other_mix, [m_two, layer_out, token_grad, sum_a[1], sum_b[1]])
    sent = n_two + m_two
    token_grad = final(me, sent, swap(sent, "mp", 1), out_two[2], flat, small[0], two * count, F32, token_grad)
    sum_a = last_sum(sum_a[0], gate(sum_a[1], [m_two]))
    sum_b = last_sum(sum_b[0], gate(sum_b[1], [m_two]))
    mix_same, mix_other, _ = finish(out_two[3], other_mix, 1, [token_grad, sum_a, sum_b])
    mix_sum = last_sum(mix_same, mix_other)
    extra = mix_sum[:, 768:896]
    gains = jnp.concatenate([extra[:, 2], extra[:, 3], extra[:each, HEAD_ROW]])
    gains = (gains + swap(gains, "mp", 1)) + (swap(gains, "mp", 2) + swap(gains, "mp", 3))
    return (
        layer_out.reshape(seq_rows, length, width),
        token_grad.reshape(seq_rows, length, width),
        gains[:depth],
        mix_sum[:, 0:256],
        mix_sum[:, 256:512],
        mix_sum[:, 512:768],
        extra[:, 0:2],
        extra[:each, TAP_ROW:HEAD_ROW].T.reshape(2, 12, each),
        gains[2 * depth :],
        mix_sum[:, 896:1152].T,
        gains[depth : 2 * depth],
        sum_a[:, :ff],
        sum_a[:, ff : 2 * ff],
        sum_b[:, :ff].T,
    )


def solution(mesh):
    return jax.shard_map(
        on_device,
        mesh=mesh,
        in_specs=(
            P("dp", None, None),
            P("dp", None),
            P("dp", None, None),
            P("dp"),
            P("dp", "mp"),
            P("dp", "mp"),
            P("dp", "mp"),
            P("dp", "mp"),
            P("mp", None, "dp"),
            P("dp"),
            P("mp", "dp"),
            P("dp"),
            P("dp", "mp"),
            P("dp", "mp"),
            P("mp", "dp"),
        ),
        out_specs=(
            P("dp", None, None),
            P("dp", None, None),
            P("dp"),
            P("dp", "mp"),
            P("dp", "mp"),
            P("dp", "mp"),
            P("dp", "mp"),
            P("mp", None, "dp"),
            P("dp"),
            P("mp", "dp"),
            P("dp"),
            P("dp", "mp"),
            P("dp", "mp"),
            P("mp", "dp"),
        ),
        check_vma=False,
    )
```

```python
import functools
import jax
import jax.numpy as jnp
from jax import lax
from jax.experimental import pallas as pl
from jax.experimental.pallas import tpu as pltpu
from jax.sharding import PartitionSpec as P

BF = jnp.bfloat16
F32 = jnp.float32
EPS = 1e-06
STEP = 256
DK = 128
VMEM_LIMIT = 58 * 1024 * 1024
FF_PAD = 768
TAP_ROW = 4
HEAD_ROW = 28
CHUNKS = 2
ORDER = (1, 0)
MLP_STEP = 512
GRAD_BLOCK = 512
TILE = 512
COST = 1.0


def nn(a, b):
    return lax.dot_general(a, b, (((1,), (0,)), ((), ())), preferred_element_type=F32)


def nt(a, b):
    return lax.dot_general(a, b, (((1,), (1,)), ((), ())), preferred_element_type=F32)


def tn(a, b):
    return lax.dot_general(a, b, (((0,), (0,)), ((), ())), preferred_element_type=F32)


def hi_lo(x):
    high = x.astype(BF)
    return high, (x - high.astype(F32)).astype(BF)


def iota(shape, dim):
    return lax.broadcasted_iota(jnp.int32, shape, dim)


def sigmoid(x):
    return 1.0 / (1.0 + jnp.exp(-x))


def keep(mask, x):
    return jnp.where(mask, x, 0.0)


def doc_starts(ends_ref, places):
    begin = jnp.zeros_like(places)
    for doc in range(ends_ref.shape[0]):
        end = ends_ref[doc]
        begin = jnp.where(places >= end, end, begin)
    return begin


def doc_masks(ends_ref, base):
    rows = doc_starts(ends_ref, base + iota((STEP, DK), 0))
    cols = doc_starts(ends_ref, base + iota((8, STEP), 1))[0:1]
    last = jnp.int32(0)
    for doc in range(ends_ref.shape[0]):
        end = ends_ref[doc]
        last = jnp.where(base + STEP - 1 >= end, end, last)
    same = jnp.concatenate([rows, rows], axis=1) == cols
    return rows, same, rows < base, rows == last, (last < base).astype(F32)


def wide_masks():
    col = iota((64, STEP), 1)
    return [(col // 64 == b).astype(F32).astype(BF) for b in range(4)]


def spread(x, masks):
    return jnp.concatenate([x * m for m in masks], axis=0)


def wide_product(a_parts, b_parts):
    (ah, al), (bh, bl) = a_parts, b_parts
    both = nn(jnp.concatenate([ah, al], axis=0), bh)
    return both[:64] + both[64:] + nn(ah, bl)


def product(a, b):
    ah, al = hi_lo(a)
    bh, bl = hi_lo(b)
    rows = a.shape[0]
    both = nn(jnp.concatenate([ah, al], axis=0), bh)
    return both[:rows] + both[rows:] + nn(ah, bl)


def inverses(lows):
    masks = wide_masks()
    row = iota((64, STEP), 0)
    col = iota((64, STEP), 1)
    inner = col % 64
    quarter = col // 64
    eye = (row == inner).astype(F32)
    n = range(len(lows))

    def split(xs):
        return [hi_lo(x) for x in xs]

    def spreads(parts):
        return [(spread(h, masks), spread(l, masks)) for h, l in parts]

    def products(a, b):
        return [wide_product(a[i], b[i]) for i in n]

    wide = []
    for low in lows:
        total = keep(quarter == 0, low[0:64])
        for b in range(1, 4):
            total = total + keep(quarter == b, low[64 * b : 64 * b + 64])
        wide.append(total)
    small = [keep(row // 8 == inner // 8, w) for w in wide]
    small_p = split(small)
    power = products(small_p, spreads(small_p))
    power_p = split(power)
    power_s = spreads(power_p)
    third = products(small_p, power_s)
    fourth = products(power_p, power_s)
    first = [eye - small[i] + power[i] - third[i] for i in n]
    more = products(split(first), spreads(split(fourth)))
    inv = [first[i] + more[i] for i in n]
    for size in (8, 16, 32):
        pair = (row // (2 * size) == inner // (2 * size)) & (row // size != inner // size)
        off_p = split([keep(pair, w) for w in wide])
        inv_p = split(inv)
        mid = products(off_p, spreads(inv_p))
        more = products(inv_p, spreads(split(mid)))
        inv = [inv[i] - more[i] for i in n]
    off_p = split([keep(quarter == 0, low[64:128]) + keep(quarter == 2, low[192:256]) for low in lows])
    inv_p = split(inv)
    mid_p = split(products(off_p, spreads(inv_p)))
    blank = jnp.zeros((64, STEP), BF)

    def shifted(x):
        return jnp.concatenate([blank, x * masks[0], blank, x * masks[2]], axis=0)

    more = products(inv_p, [(shifted(h), shifted(l)) for h, l in mid_p])
    top, bottom = [], []
    for i in n:
        t, q = inv[i], more[i]
        top.append(
            jnp.concatenate(
                [keep(quarter == 0, t)[:, :128], (keep(quarter == 1, t) - keep(quarter == 0, q))[:, :128]], axis=0
            )
        )
        bottom.append(
            jnp.concatenate(
                [keep(quarter == 2, t)[:, 128:], (keep(quarter == 3, t) - keep(quarter == 2, q))[:, 128:]], axis=0
            )
        )
    mid = [product(lows[i][128:, :128], top[i]) for i in n]
    corner = [product(bottom[i], mid[i]) for i in n]
    blank = jnp.zeros((128, 128), F32)
    return [
        jnp.concatenate(
            [jnp.concatenate([top[i], blank], axis=1), jnp.concatenate([-corner[i], bottom[i]], axis=1)], axis=0
        )
        for i in n
    ]


def conv_of(buffer_ref, taps_ref, part, reach, base_row):
    branch, head = divmod(part, 2)
    lanes = slice(part * DK, (part + 1) * DK)
    first = TAP_ROW + head * 12 + branch * 4
    total = buffer_ref[base_row : base_row + STEP, lanes] * taps_ref[first + 3 : first + 4, :]
    for behind in range(1, 4):
        moved = buffer_ref[base_row - behind : base_row - behind + STEP, lanes]
        tap = first + 3 - behind
        total = total + keep(reach[behind], moved * taps_ref[tap : tap + 1, :])
    return total


def tn_product(a, b):
    ah, al = hi_lo(a)
    bh, bl = hi_lo(b)
    both = tn(ah, jnp.concatenate([bh, bl], axis=1))
    n = b.shape[1]
    return both[:, :n] + both[:, n:] + tn(al, bh)


def col_sum(x):
    return jnp.sum(x, axis=0, keepdims=True)


def whole(*shape):
    return pl.BlockSpec(shape, lambda *_: (0,) * len(shape))


def sds(shape, kind):
    return jax.ShapeDtypeStruct(shape, kind)


def any_ref():
    return pl.BlockSpec(memory_space=pl.ANY)


def call(kernel, args, after, prefetch, grid, in_specs, out_specs, out_shape, scratch, micros):
    given = len(args)

    def body(*refs):
        return kernel(*refs[:given], *refs[given + len(after) :])

    return pl.pallas_call(
        body,
        grid_spec=pltpu.PrefetchScalarGridSpec(
            num_scalar_prefetch=prefetch, grid=grid, in_specs=list(in_specs) + [any_ref()] * len(after),
            out_specs=out_specs, scratch_shapes=scratch,
        ),
        out_shape=out_shape,
        compiler_params=pltpu.CompilerParams(vmem_limit_bytes=VMEM_LIMIT),
        cost_estimate=pl.CostEstimate(flops=int(micros * 8e8 * COST), bytes_accessed=0, transcendentals=0),
    )(*args, *after)


def shard_copies(own, shards, lanes, target, sems, depth):
    copies = []
    for k, shard in enumerate(shards):
        row = pl.multiple_of((own ^ k) * depth, depth)
        copies.append(pltpu.make_async_copy(shard.at[:, lanes], target.at[pl.ds(row, depth), :], sems.at[k]))
    return copies


def run_copies(copies):
    for copy in copies:
        copy.start()
    for copy in copies:
        copy.wait()


def slot(index, count):
    out = 0
    while count > 1:
        out, index, count = out * 2 + index % 2, index // 2, count // 2
    return out


def feature_rows(shards, depth):
    each = DK // shards
    row = iota((depth * shards, DK), 0)
    col = iota((depth * shards, DK), 1)
    inside = row % depth
    return ((inside < each) & ((row // depth) * each + inside == col)).astype(F32).astype(BF)


def mixer_fwd_kernel(*refs, first_row, shards, depth, width):
    step = pl.program_id(0)
    if shards:
        me_ref, ends_ref, tok_ref = refs[:3]
        shard_refs, refs = refs[3 : 3 + shards], refs[3 + shards :]
        outs, (buffer, state, sems) = refs[:15], refs[15:]
        w_ref, gain_ref, taps_ref, s_out_ref, halo_out_ref = outs[10:]
        outs = outs[:10]
    else:
        me_ref, ends_ref, tok_ref, w_ref, gain_ref, taps_ref, s_in_ref, halo_ref = refs[:8]
        outs, s_out_ref, halo_out_ref, (buffer, state) = refs[8:18], refs[18], refs[19], refs[20:]
    proj_ref, qkv_ref, beta_ref, mixed_ref, normed_ref, inv_ref, wu_ref, r_ref, pm_ref, state_ref = outs
    base = first_row + step * STEP

    @pl.when(step == 0)
    def _():
        if shards:
            copies = shard_copies(me_ref[0], shard_refs, slice(0, 896), w_ref, sems.at[0], depth)
            copies += shard_copies(me_ref[0], shard_refs, slice(896, 1152), normed_ref, sems.at[1], depth)
            run_copies(copies)
            extra = w_ref[:, 768:896]
            pick = (iota((8, DK), 1) == iota((8, DK), 0) + 2).astype(F32).astype(BF)
            gain_ref[...] = nt(pick, extra)
            taps_ref[...] = tn(extra, feature_rows(shards, depth))[:32]
            state[...] = jnp.zeros_like(state)
            buffer[0:8, :] = jnp.zeros((8, 768), F32)
        else:
            state[...] = s_in_ref[...]
            buffer[0:8, :] = halo_ref[...]

    tok = tok_ref[...].astype(F32)
    scale = lax.rsqrt(jnp.mean(tok * tok, axis=-1, keepdims=True) + EPS)
    low_in = (tok * scale * gain_ref[0:1, :]).astype(BF)
    proj = nn(low_in, w_ref[...])
    buffer[8 : 8 + STEP, :] = proj[:, :768]
    proj_ref[...] = proj[:, :768]
    betas = sigmoid(proj[:, 768:896])
    beta_ref[...] = betas
    beta_t = betas.T
    rows, same, carry, in_last, go_on = doc_masks(ends_ref, base)
    behind = base + iota((STEP, DK), 0) - rows
    reach = [None] + [behind >= s for s in (1, 2, 3)]
    parts = []
    for part in range(6):
        pre = conv_of(buffer, taps_ref, part, reach, 8)
        act = pre * sigmoid(pre)
        if part < 4:
            norm = lax.rsqrt(jnp.sum(act * act, axis=-1, keepdims=True) + EPS)
            act = act * norm
            if part < 2:
                act = act * DK**-0.5
        parts.append(act.astype(BF))
    halo_out_ref[...] = buffer[STEP : STEP + 8, :]
    buffer[0:8, :] = buffer[STEP : STEP + 8, :]
    qkv_ref[...] = jnp.concatenate(parts, axis=1)
    at_row = iota((STEP, STEP), 0)
    at_col = iota((STEP, STEP), 1)
    strict = same & (at_row > at_col)
    lower = same & (at_row >= at_col)
    heads = range(2)
    q, k, v = parts[0:2], parts[2:4], parts[4:6]
    lows = [keep(strict, nt(k[h], k[h]) * betas[:, h : h + 1]) for h in heads]
    invs = inverses(lows)
    head_gain = taps_ref[HEAD_ROW : HEAD_ROW + 1, :]
    def one_head(h):
        inv_ref[0, h] = invs[h].astype(BF)
        scaled_h, scaled_l = hi_lo(invs[h] * beta_t[h : h + 1, :])
        yield
        kv = jnp.concatenate([k[h], v[h]], axis=1)
        solved = nn(scaled_h, kv) + nn(scaled_l, kv)
        wu_ref[0, h] = solved.astype(BF)
        yield
        w = keep(carry, solved[:, :DK])
        both_h, both_l = hi_lo(jnp.concatenate([solved[:, DK:], w], axis=1))
        scores = keep(lower, nt(q[h], k[h])).astype(BF)
        yield
        inside = nn(scores, both_h)
        k_last = keep(in_last, k[h].astype(F32)).astype(BF)
        outer = tn(k_last, both_h) + tn(k_last, both_l)
        yield
        r = (keep(carry, q[h].astype(F32)) - inside[:, DK:]).astype(BF)
        r_ref[0, h] = r
        pm_ref[0, h] = outer[:, DK:]
        now = state[h]
        now_h, now_l = hi_lo(now)
        state_ref[0, h] = now_h
        yield
        out = nn(r, jnp.concatenate([now_h, now_l], axis=1))
        yield
        mixed = inside[:, :DK] + out[:, :DK] + out[:, DK:]
        state[h] = go_on * now - product(outer[:, DK:], now) + outer[:, :DK]
        yield
        lanes = slice(h * DK, (h + 1) * DK)
        mixed_ref[:, lanes] = mixed
        scale = lax.rsqrt(jnp.mean(mixed * mixed, axis=-1, keepdims=True) + EPS)
        head_normed = (mixed * scale * head_gain).astype(BF)
        if shards:
            normed_ref[pl.ds(pl.multiple_of(width + step * STEP, STEP), STEP), lanes] = head_normed
        else:
            normed_ref[:, lanes] = head_normed
        yield

    running = [one_head(0), one_head(1)]
    while running:
        running = [r for r in running if next(r, r) is not r]
    s_out_ref[...] = state[...]


def mixer_fwd(me, ends, tokens, count, first_row, after=(), shards=None, w_in=None, small=None, carried=None):
    width = tokens.shape[1]
    steps = count // STEP
    start = first_row // STEP
    rows = lambda n, at=0: pl.BlockSpec((STEP, n), lambda i: (i + at, 0))
    group = lambda *s: pl.BlockSpec((1,) + s, lambda i: (i,) + (0,) * len(s))
    smem = pl.BlockSpec(memory_space=pltpu.SMEM)
    out_specs = [
        rows(768), rows(768), rows(DK), rows(256), rows(256),
        group(2, STEP, STEP), group(2, STEP, STEP), group(2, STEP, DK), group(2, DK, DK), group(2, DK, DK),
    ]
    out_shape = [
        sds((count, 768), F32), sds((count, 768), BF), sds((count, DK), F32), sds((count, 256), F32),
        sds((count, 256), BF), sds((steps, 2, STEP, STEP), BF), sds((steps, 2, STEP, STEP), BF),
        sds((steps, 2, STEP, DK), BF), sds((steps, 2, DK, DK), F32), sds((steps, 2, DK, DK), BF),
    ]
    scratch = [pltpu.VMEM((STEP + 8, 768), F32), pltpu.VMEM((2, DK, DK), F32)]
    if shards:
        args = [me, ends, tokens, *shards]
        in_specs = [smem, smem, rows(width, start)] + [any_ref()] * len(shards)
        out_specs[4] = whole(width + count, 256)
        out_shape[4] = sds((width + count, 256), BF)
        out_specs += [whole(width, 896), whole(8, width), whole(32, DK)]
        out_shape += [sds((width, 896), BF), sds((8, width), F32), sds((32, DK), F32)]
        scratch.append(pltpu.SemaphoreType.DMA((2, len(shards))))
    else:
        args = [me, ends, tokens, w_in, *small, *carried]
        in_specs = [
            smem, smem, rows(width, start), whole(width, 896), whole(8, width), whole(32, DK),
            whole(2, DK, DK), whole(8, 768),
        ]
    out_specs += [whole(2, DK, DK), whole(8, 768)]
    out_shape += [sds((2, DK, DK), F32), sds((8, 768), F32)]
    return call(
        functools.partial(
            mixer_fwd_kernel, first_row=first_row, shards=len(shards) if shards else 0,
            depth=shards[0].shape[0] if shards else 0, width=width,
        ),
        args, after, 0, (steps,), in_specs, out_specs, out_shape, scratch, 6 * steps,
    )


def mixer_bwd_kernel(*refs, first_row, steps, first, last, shards, depth):
    step = pl.program_id(0)
    (
        me_ref, ends_ref, mine_ref, theirs_ref, res_ref, cot_ref, tok_ref, proj_ref, prev_ref, before_ref, qkv_ref, beta_ref, mixed_ref, normed_ref,
        inv_ref, wu_ref, r_ref, pm_ref, state_ref, w_ref, wo_ref, gain_ref, taps_ref,
    ) = refs[:23]
    refs = refs[23:]
    if not first:
        gw_in, gwo_in, gsmall_in, gnorm_in, ds_in_ref, halo_ref = refs[:6]
        refs = refs[6:]
    if last:
        ggain_refs, refs = refs[:2], refs[2:]
    dn_mine, dn_theirs, d_att_ref = refs[:3]
    refs = refs[3:]
    if last:
        same_ref, other_ref, refs = refs[0], refs[1], refs[2:]
    else:
        out_refs, refs = refs[:6], refs[6:]
    buffer, ahead, dstate, back_s, gw_ref, gwo_ref, gsmall_ref, gnorm_ref = refs
    tile = steps - 1 - step
    base = first_row + tile * STEP
    half = tile // (steps // 2)
    core = me_ref[1] & 1

    @pl.when(step == 0)
    def _():
        if first:
            dstate[...] = jnp.zeros_like(dstate)
            ahead[:, 0:8, :] = jnp.zeros((3, 8, 768), F32)
            gw_ref[...] = jnp.zeros_like(gw_ref)
            gwo_ref[...] = jnp.zeros_like(gwo_ref)
            gsmall_ref[...] = jnp.zeros_like(gsmall_ref)
            gnorm_ref[...] = jnp.zeros_like(gnorm_ref)
        else:
            dstate[...] = ds_in_ref[...]
            ahead[:, 0:8, :] = halo_ref[...]
            gw_ref[...] = gw_in[...]
            gwo_ref[...] = gwo_in[...]
            gsmall_ref[...] = gsmall_in[...]
            gnorm_ref[...] = gnorm_in[...]

    @pl.when(half == core)
    def _():
        back_s[...] = mine_ref[...]

    @pl.when(half != core)
    def _():
        back_s[...] = theirs_ref[...]

    ahead[:, STEP : STEP + 8, :] = ahead[:, 0:8, :]
    d_resid = cot_ref[...].astype(F32) + norm_back(back_s[...].astype(F32), res_ref[...], gain_ref[1:2, :])
    d_att = d_resid.astype(BF)
    d_att_ref[...] = d_att
    d_head = nn(d_att, wo_ref[...])
    gwo_ref[...] += tn(d_att, normed_ref[...])
    rows, same, carry, in_last, go_on = doc_masks(ends_ref, base)
    at_row = iota((STEP, STEP), 0)
    at_col = iota((STEP, STEP), 1)
    strict = same & (at_row > at_col)
    lower = same & (at_row >= at_col)
    strict_t = same & (at_row < at_col)
    lower_t = same & (at_row <= at_col)
    betas = beta_ref[...]
    beta_t = betas.T
    heads = range(2)
    d_mixer = [None] * 6
    lane = iota((STEP, DK), 1)
    head_gain = taps_ref[HEAD_ROW : HEAD_ROW + 1, :]
    d_beta = [None, None]

    def one_head(h):
        lanes = slice(h * DK, (h + 1) * DK)
        mixed = mixed_ref[:, lanes]
        e = d_head[:, lanes]
        scale = lax.rsqrt(jnp.mean(mixed * mixed, axis=-1, keepdims=True) + EPS)
        unit = mixed * scale
        gain_part[h] = col_sum(e * unit)
        ge = e * head_gain
        d_out = (scale * (ge - unit * jnp.mean(unit * ge, axis=-1, keepdims=True))).astype(BF)
        yield
        q = qkv_ref[:, h * DK : (h + 1) * DK]
        k = qkv_ref[:, 256 + h * DK : 256 + (h + 1) * DK]
        v = qkv_ref[:, 512 + h * DK : 512 + (h + 1) * DK]
        wu = wu_ref[0, h]
        inv = inv_ref[0, h]
        r = r_ref[0, h]
        s_in = state_ref[0, h]
        beta_col = betas[:, h : h + 1]
        beta_row = beta_t[h : h + 1, :]
        dst = dstate[h]
        ds_h = dst.astype(BF)
        dstate[h] = go_on * dst - tn_product(pm_ref[0, h], dst) + tn(r, d_out)
        scores_t = keep(lower_t, nt(k, q)).astype(BF)
        yield
        k_last = keep(in_last, k.astype(F32)).astype(BF)
        d_x = nn(scores_t, d_out) + nn(k_last, ds_h)
        yield
        carried_w = keep(carry, wu[:, :DK].astype(F32)).astype(BF)
        x = (wu[:, DK:].astype(F32) - nn(carried_w, s_in)).astype(BF)
        yield
        d_xb = d_x.astype(BF)
        d_scores = keep(lower, nt(d_out, x)).astype(BF)
        d_scores_t = keep(lower_t, nt(x, d_out)).astype(BF)
        yield
        back_s = nt(jnp.concatenate([d_out, d_xb], axis=0), s_in)
        d_q = keep(carry, back_s[:STEP]) + nn(d_scores, k)
        d_k = nn(d_scores_t, q) + keep(in_last, nt(x, ds_h))
        yield
        d_w = -keep(carry, back_s[STEP:])
        z = tn(inv, jnp.concatenate([d_w.astype(BF), d_xb], axis=1))
        yield
        z_b = z.astype(BF)
        d_a = -keep(strict, nt(z_b, wu))
        d_a_t = -keep(strict_t, nt(wu, z_b))
        yield
        gram = nt(k, k)
        kv = jnp.concatenate([k, v], axis=1).astype(F32)
        yield
        d_b = jnp.sum(d_a * gram + z * kv, axis=-1, keepdims=True)
        d_g = (d_a * beta_col + d_a_t * beta_row).astype(BF)
        d_k = d_k + nn(d_g, k) + beta_col * z[:, :DK]
        d_v = beta_col * z[:, DK:]
        for place, grad in ((h, d_q), (2 + h, d_k), (4 + h, d_v)):
            d_mixer[place] = grad.astype(BF).astype(F32)
        d_beta[h] = d_b * beta_col * (1.0 - beta_col)
        yield

    before = before_ref[...] if first_row else jnp.zeros((8, 768), F32)
    buffer[0:8, :] = jnp.where(tile == 0, before, prev_ref[...])
    buffer[8 : 8 + STEP, :] = proj_ref[...]
    behind = base + iota((STEP, DK), 0) - rows
    reach = [None] + [behind >= s for s in (1, 2, 3)]
    slopes, norms, units = [None] * 6, [None] * 6, [None] * 6

    def convs():
        for part in range(6):
            pre = conv_of(buffer, taps_ref, part, reach, 8)
            sig = sigmoid(pre)
            slopes[part] = sig * (1.0 + pre * (1.0 - sig))
            if part < 4:
                act = pre * sig
                norms[part] = lax.rsqrt(jnp.sum(act * act, axis=-1, keepdims=True) + EPS)
                units[part] = act * norms[part]
            yield

    gain_part = [None, None]
    running = [one_head(0), one_head(1), convs()]
    while running:
        running = [r for r in running if next(r, r) is not r]
    gsmall_ref[HEAD_ROW : HEAD_ROW + 1, :] += gain_part[0] + gain_part[1]
    d_beta = jnp.where(lane == 0, d_beta[0], jnp.where(lane == 1, d_beta[1], 0.0))
    d_proj = []
    for part in range(6):
        branch, head = divmod(part, 2)
        lanes = slice(part * DK, (part + 1) * DK)
        tap0 = TAP_ROW + head * 12 + branch * 4
        grad = d_mixer[part]
        if part < 4:
            unit = units[part]
            grad = norms[part] * (grad - unit * jnp.sum(unit * grad, axis=-1, keepdims=True))
            if part < 2:
                grad = grad * DK**-0.5
        grad = grad * slopes[part]
        d_in = grad * taps_ref[tap0 + 3 : tap0 + 4, :]
        gsmall_ref[tap0 + 3 : tap0 + 4, :] += col_sum(grad * buffer[8 : 8 + STEP, lanes])
        for s in (1, 2, 3):
            tap = tap0 + 3 - s
            masked = keep(reach[s], grad)
            gsmall_ref[tap : tap + 1, :] += col_sum(masked * buffer[8 - s : 8 - s + STEP, lanes])
            ahead[s - 1, 0:STEP, lanes] = masked
            d_in = d_in + ahead[s - 1, s : s + STEP, lanes] * taps_ref[tap : tap + 1, :]
        d_proj.append(d_in.astype(BF))
    d_proj.append(d_beta.astype(BF))
    d_proj = jnp.concatenate(d_proj, axis=1)
    tok = tok_ref[...].astype(F32)
    unit = tok * lax.rsqrt(jnp.mean(tok * tok, axis=-1, keepdims=True) + EPS)
    low_in = (unit * gain_ref[0:1, :]).astype(BF)
    gw_ref[...] += tn(low_in, d_proj)
    d_normed = nt(d_proj, w_ref[...])
    gnorm_ref[0:1, :] += col_sum(d_normed * unit)

    @pl.when(half == core)
    def _():
        dn_mine[...] = d_normed.astype(BF)

    @pl.when(half != core)
    def _():
        dn_theirs[...] = d_normed.astype(BF)

    @pl.when(step == steps - 1)
    def _():
        if last:
            small = jnp.concatenate([gsmall_ref[...], jnp.zeros((DK - 32, DK), F32)], axis=0).astype(BF)
            gnorm_ref[1:2, :] = ggain_refs[0][0:1, :] + ggain_refs[1][0:1, :]
            spot = (iota((8, DK), 1) == 2 + iota((8, DK), 0)) & (iota((8, DK), 0) < 2)
            extra = tn(gnorm_ref[...].astype(BF), spot.astype(F32).astype(BF))
            gw_ref[:, 768:896] += nt(feature_rows(shards, depth), small) + extra
            for k in range(shards):
                row = pl.multiple_of((me_ref[0] ^ k) * depth, depth)
                target = same_ref if k % 2 == 0 else other_ref
                place = slot(k // 2, shards // 2)
                target[place, :, 0:896] = gw_ref[pl.ds(row, depth), :].astype(BF)
                target[place, :, 896:1152] = gwo_ref[pl.ds(row, depth), :].astype(BF)
        else:
            for out, value in zip(out_refs, (gw_ref, gwo_ref, gsmall_ref, gnorm_ref, dstate)):
                out[...] = value[...]
            out_refs[5][...] = ahead[:, 0:8, :]


def mixer_bwd(me, ends, mine, theirs, res, cot, tokens, saved, w_in, wo_own, small, first_row, carried, last, shards, after=(), ggain=None):
    proj, qkv, betas, mixed, normed, inv, wu, r, pm, states, prev, normed_at = saved
    count, width = proj.shape[0], tokens.shape[1]
    steps = count // STEP
    per_half = steps // 2
    start = first_row // STEP
    rows = lambda n, at=0: pl.BlockSpec((STEP, n), lambda i, me: (steps - 1 - i + at, 0))
    group = lambda *s: pl.BlockSpec((1,) + s, lambda i, me: (steps - 1 - i,) + (0,) * len(s))

    def half_rows(flip):
        def place(i, me):
            tile = steps - 1 - i
            half, inside = tile // per_half, tile % per_half
            wanted = (me[1] & 1) ^ flip
            return (jnp.where(half == wanted, inside, jnp.where(half > wanted, per_half - 1, 0)), 0)

        return pl.BlockSpec((STEP, width), place)

    in_specs = [
        pl.BlockSpec(memory_space=pltpu.SMEM), half_rows(0), half_rows(1), rows(width), rows(width, start), rows(width, start), rows(768),
        pl.BlockSpec((8, 768), lambda i, me: (jnp.maximum((steps - 1 - i) * (STEP // 8) - 1, 0), 0)),
        whole(8, 768), rows(768), rows(DK), rows(256), rows(256, normed_at),
        group(2, STEP, STEP), group(2, STEP, STEP), group(2, STEP, DK), group(2, DK, DK), group(2, DK, DK),
        whole(width, 896), whole(width, 256), whole(8, width), whole(32, DK),
    ]
    args = [
        me, ends, mine, theirs, res, cot, tokens, proj, proj, prev, qkv, betas, mixed, normed, inv, wu, r, pm, states, w_in, wo_own,
        *small,
    ]
    sums = [(width, 896), (width, 256), (32, DK), (8, width), (2, DK, DK), (3, 8, 768)]
    if carried is not None:
        args += carried
        in_specs += [whole(*s) for s in sums]
    if last:
        args += ggain
        in_specs += [whole(8, width)] * 2
    depth = width // shards
    out_specs = [half_rows(0), half_rows(1), rows(width)]
    out_shape = [sds((count // 2, width), BF)] * 2 + [sds((count, width), BF)]
    if last:
        out_specs += [whole(shards // 2, depth, 1152)] * 2
        out_shape += [sds((shards // 2, depth, 1152), BF)] * 2
    else:
        out_specs += [whole(*s) for s in sums]
        out_shape += [sds(s, F32) for s in sums]
    return call(
        functools.partial(
            mixer_bwd_kernel, first_row=first_row, steps=steps, first=carried is None, last=last, shards=shards,
            depth=depth,
        ),
        args, after, 1, (steps,), in_specs, out_specs, out_shape,
        [
            pltpu.VMEM((STEP + 8, 768), F32), pltpu.VMEM((3, STEP + 8, 768), F32), pltpu.VMEM((2, DK, DK), F32),
            pltpu.VMEM((STEP, width), BF), pltpu.VMEM((width, 896), F32), pltpu.VMEM((width, 256), F32),
            pltpu.VMEM((32, DK), F32), pltpu.VMEM((8, width), F32),
        ],
        7 * steps,
    )


def mlp_kernel(*refs, steps, shards, depth, ff):
    step = pl.program_id(0)
    me_ref, tok_ref, cot_ref, gain_ref = refs[:4]
    head_refs, refs = refs[4:8], refs[8:]
    if shards:
        shard_refs, wo_refs, refs = refs[:shards], refs[shards : shards + 4], refs[shards + 4 :]
    else:
        g_ref, u_ref, d_ref, wo_ref = refs[:4]
        refs = refs[4:]
    back_mine, back_theirs, down_mine, down_theirs, res_ref, normed_ref, act_ref, dg_ref, du_ref, ggain_ref = refs[:10]
    refs = refs[10:]
    if shards:
        g_ref, u_ref, d_ref, wo_ref, heads, raw, sems, wo_sems = refs
    else:
        (heads,) = refs
    own = me_ref[1]

    @pl.when(step == 0)
    def _():
        ggain_ref[...] = jnp.zeros_like(ggain_ref)
        if shards:
            copies = shard_copies(me_ref[0], shard_refs, slice(None), raw, sems, depth)
            width = raw.shape[0]
            copies += [pltpu.make_async_copy(wo_refs[m].at[pl.ds(0, width), :], wo_ref.at[own ^ m], wo_sems.at[m]) for m in range(4)]
            run_copies(copies)
            inside = iota((256, FF_PAD), 1) < ff
            for at in range(0, raw.shape[0], 256):
                here = slice(at, at + 256)
                g_ref[here, :] = keep(inside, raw[here, 0:FF_PAD].astype(F32)).astype(BF)
                from_u = ff - ff % 128
                turned = pltpu.roll(
                    raw[here, from_u : from_u + FF_PAD].astype(F32), FF_PAD - ff % 128, axis=1
                )
                u_ref[here, :] = keep(inside, turned).astype(BF)
                from_d = 2 * ff
                d_ref[here, :] = keep(inside, raw[here, from_d : from_d + FF_PAD].astype(F32)).astype(BF)

    for m in range(4):
        heads[own ^ m] = head_refs[m][...]
    attended = nt(heads[0], wo_ref[0])
    for m in range(1, 4):
        attended = attended + nt(heads[m], wo_ref[m])
    res = tok_ref[...].astype(F32) + attended
    res_ref[...] = res
    unit = res * lax.rsqrt(jnp.mean(res * res, axis=-1, keepdims=True) + EPS)
    normed = (unit * gain_ref[1:2, :]).astype(BF)
    normed_ref[...] = normed
    gate = nn(normed, g_ref[...])
    up = nn(normed, u_ref[...])
    sig = sigmoid(gate)
    silu = gate * sig
    act = (silu * up).astype(BF)
    act_ref[...] = act
    d_hidden = nn(cot_ref[...], d_ref[...])
    d_gate = (d_hidden * up * sig * (1.0 + gate * (1.0 - sig))).astype(BF)
    d_up = (d_hidden * silu).astype(BF)
    dg_ref[...] = d_gate
    du_ref[...] = d_up
    down = nt(act, d_ref[...]).astype(BF)
    back = nt(d_gate, g_ref[...]) + nt(d_up, u_ref[...])
    ggain_ref[0:1, :] += col_sum(back * unit)

    @pl.when(step < steps // 2)
    def _():
        back_theirs[...] = back.astype(BF)
        down_theirs[...] = down

    @pl.when(step >= steps // 2)
    def _():
        back_mine[...] = back.astype(BF)
        down_mine[...] = down


def mlp(me, tokens, cot, small, heads, heads_at, count, first_row, ff, after=(), shards=None, wo=None, weights=None):
    width = tokens.shape[1]
    steps = count // STEP
    per_half = steps // 2
    start = first_row // STEP

    def tile(i, me, at=0):
        half = jnp.where(i >= per_half, me[1] & 1, 1 - (me[1] & 1))
        return at + half * per_half + i % per_half

    rows = lambda n, at=0: pl.BlockSpec((STEP, n), lambda i, me: (tile(i, me, at), 0))
    theirs = pl.BlockSpec((STEP, width), lambda i, me: (jnp.minimum(i, per_half - 1), 0))
    mine = pl.BlockSpec((STEP, width), lambda i, me: (jnp.maximum(i - per_half, 0), 0))
    in_specs = [rows(width, start), rows(width, start), whole(8, width)] + [rows(256, heads_at)] * 4
    args = [me, tokens, cot, small[0], *heads]
    out_specs = [mine, theirs, mine, theirs, rows(width), rows(width), rows(FF_PAD), rows(FF_PAD), rows(FF_PAD), whole(8, width)]
    halves = (count // 2, width)
    out_shape = [
        sds(halves, BF), sds(halves, BF), sds(halves, BF), sds(halves, BF), sds((count, width), F32), sds((count, width), BF),
        sds((count, FF_PAD), BF), sds((count, FF_PAD), BF), sds((count, FF_PAD), BF), sds((8, width), F32),
    ]
    kept = [(width, FF_PAD)] * 3 + [(4, width, 256)]
    scratch = [pltpu.VMEM((4, STEP, 256), BF)]
    if shards:
        in_specs += [any_ref()] * (len(shards) + 4)
        args += [*shards, *wo]
        out_specs += [whole(*s) for s in kept]
        out_shape += [sds(s, BF) for s in kept]
        scratch += [
            pltpu.VMEM((width, shards[0].shape[1]), BF),
            pltpu.SemaphoreType.DMA((len(shards),)), pltpu.SemaphoreType.DMA((4,)),
        ]
    else:
        in_specs += [whole(*s) for s in kept]
        args += weights
    return call(
        functools.partial(
            mlp_kernel, steps=steps, shards=len(shards) if shards else 0, depth=shards[0].shape[0] if shards else 0,
            ff=ff,
        ),
        args, after, 1, (steps,), in_specs, out_specs, out_shape, scratch, 6 * steps,
    )


def mlp_grads_kernel(me_ref, *refs, chunks, shards, depth, ff):
    step = pl.program_id(0)
    left, refs = refs[:chunks], refs[chunks:]
    rights, (same, other, packed) = refs[:-3], refs[-3:]
    each = 256 // depth

    def over_rows(right):
        total = tn(left[0][...], right[0][...])
        for a, b in zip(left[1:], right[1:]):
            total = total + tn(a[...], b[...])
        return total

    first = over_rows(rights[:chunks])
    if len(rights) == chunks:
        packed[...] = first
    else:
        cut = ff - ff % 128
        turned = pltpu.roll(over_rows(rights[chunks:]), ff % 128, axis=1)
        packed[:, 0:cut] = first[:, 0:cut]
        packed[:, cut : cut + 128] = first[:, cut : cut + 128] + turned[:, 0:128]
        packed[:, cut + 128 : 2 * ff] = turned[:, 128 : 2 * ff - cut]
    for i in range(shards // each):

        @pl.when(step == i)
        def _(i=i):
            for t in range(each):
                row = pl.multiple_of((t ^ (me_ref[0] % each)) * depth, depth)
                k = i * each + t
                (same if k % 2 == 0 else other)[slot(k // 2, shards // 2)] = packed[pl.ds(row, depth), :].astype(BF)


def mlp_grads(me, left, left_at, rights, shards, ff, after=()):
    chunks = len(left)
    count, width = rights[0].shape[0], left[0].shape[1]
    depth = width // shards
    each = 256 // depth
    column = lambda at: pl.BlockSpec((count, 256), lambda i, me: (at, (me[0] // each) ^ i))
    wide = FF_PAD if len(rights) == chunks else 2 * ff
    stack = (shards // 2, depth, wide)
    return call(
        functools.partial(mlp_grads_kernel, chunks=chunks, shards=shards, depth=depth, ff=ff),
        (me, *left, *rights), after, 1, (width // 256,),
        [column(at) for at in left_at] + [whole(count, FF_PAD)] * len(rights),
        [whole(*stack)] * 2, [sds(stack, BF)] * 2, [pltpu.VMEM((256, wide), F32)], 6,
    )


def norm_back(e, v, gain):
    scale = lax.rsqrt(jnp.mean(v * v, axis=-1, keepdims=True) + EPS)
    unit = v * scale
    ge = e * gain
    return scale * (ge - unit * jnp.mean(unit * ge, axis=-1, keepdims=True))


def pair_kernel(own_ref, other_ref, out_ref):
    out_ref[...] = own_ref[...] + other_ref[...]


def pair_after(own, other, after):
    vmem = pl.BlockSpec(memory_space=pltpu.VMEM)
    return call(pair_kernel, (own, other), after, 0, (), [vmem] * 2, vmem, sds(own.shape, BF), [], 2)


def split_pair_kernel(own_ref, other_ref, *out_refs):
    rows = out_refs[0].shape[0]
    for i, out_ref in enumerate(out_refs):
        here = slice(i * rows, (i + 1) * rows)
        out_ref[...] = own_ref[here, :] + other_ref[here, :]


def split_pair_after(own, other, after):
    vmem = pl.BlockSpec(memory_space=pltpu.VMEM)
    part = sds((own.shape[0] // 2, own.shape[1]), BF)
    return call(split_pair_kernel, (own, other), after, 0, (), [vmem] * 2, [vmem] * 2, [part] * 2, [], 2)


def gate(x, after):
    return pl.pallas_call(
        lambda *refs: None,
        in_specs=[any_ref()] * (1 + len(after)),
        out_specs=any_ref(),
        out_shape=sds(x.shape, x.dtype),
        input_output_aliases={0: 0},
        cost_estimate=pl.CostEstimate(flops=0, bytes_accessed=0, transcendentals=0),
    )(x, *after)


def final_kernel(me_ref, mine_ref, theirs_ref, base_ref, tok_ref, gain_ref, *refs):
    out_ref, moved = refs[-2:]
    first = pl.program_id(0) < pl.num_programs(0) // 2
    low_core = (me_ref[1] & 1) == 0

    @pl.when(first == low_core)
    def _():
        moved[...] = mine_ref[...]

    @pl.when(first != low_core)
    def _():
        moved[...] = theirs_ref[...]

    part = moved[...].astype(F32)
    if out_ref.dtype == F32:
        part = norm_back(part, tok_ref[...].astype(F32), gain_ref[0:1, :])
    out_ref[...] = (base_ref[...].astype(F32) + part).astype(out_ref.dtype)


def final(me, mine, theirs, base, tokens, gain, first_row, kind, into=None):
    count, width = base.shape
    size = TILE
    tiles = count // 2 // size
    start = first_row // size

    def half_rows(flip):
        def place(i, me):
            half, inside = i // tiles, i % tiles
            wanted = (me[1] & 1) ^ flip
            return (jnp.where(half == wanted, inside, jnp.where(half > wanted, tiles - 1, 0)), 0)

        return pl.BlockSpec((size, width), place)

    rows = lambda at: pl.BlockSpec((size, width), lambda i, me: (at + i, 0))
    args = [me, mine, theirs, base, tokens, gain]
    in_specs = [half_rows(0), half_rows(1), rows(0), rows(start) if kind == F32 else rows(start), whole(8, width)]
    if into is not None:
        args.append(into)
        in_specs.append(any_ref())
    return pl.pallas_call(
        final_kernel,
        grid_spec=pltpu.PrefetchScalarGridSpec(
            num_scalar_prefetch=1, grid=(2 * tiles,), in_specs=in_specs, out_specs=rows(start),
            scratch_shapes=[pltpu.VMEM((size, width), BF)],
        ),
        out_shape=sds(tokens.shape, kind),
        input_output_aliases={6: 0} if into is not None else {},
        compiler_params=pltpu.CompilerParams(vmem_limit_bytes=VMEM_LIMIT),
        cost_estimate=pl.CostEstimate(flops=int(1e9 * COST), bytes_accessed=0, transcendentals=0),
    )(*args)


def swap(x, axis, k):
    return lax.ppermute(x, axis, [(i, i ^ k) for i in range(lax.axis_size(axis))])


def pair_sum(own, other):
    return own + other


def finish(same, other, bit, after=()):
    sent = other
    while same.shape[0] > 1:
        half = same.shape[0] // 2
        same, sent = same[:half] + other[:half], same[half:] + other[half:]
        bit *= 2
        other = swap(sent, "dp", bit)
        if after:
            other, after = gate(other, after), ()
    return same, other, sent


def last_sum(same, other):
    return same[0].astype(F32) + other[0].astype(F32)


def on_device(
    tokens, doc_lengths, cotangent, norm_gain, w_query, w_key, w_value, w_beta, conv_taps, head_gain, w_out, mlp_gain,
    w_gate, w_up, w_down,
):
    seq_rows, length, width = tokens.shape
    shards = lax.axis_size("dp")
    depth = width // shards
    each = conv_taps.shape[2]
    ff = w_gate.shape[1]
    me = jnp.stack([lax.axis_index("dp"), lax.axis_index("mp")]).astype(jnp.int32)
    ends = jnp.cumsum(doc_lengths[0]).astype(jnp.int32)
    flat = tokens.reshape(length, width)
    cot = cotangent.reshape(length, width)
    tall = lambda x: jnp.pad(x, ((0, depth - x.shape[0]), (0, 0)))
    pack = jnp.concatenate(
        [
            w_query, w_key, w_value, w_beta, norm_gain[:, None], mlp_gain[:, None],
            tall(conv_taps.reshape(24, each).T), tall(head_gain[:, None]), jnp.zeros((depth, 99), BF), w_out.T,
        ],
        axis=1,
    )
    total = length
    count = length // CHUNKS
    far = [swap(pack, "dp", k) for k in range(2, shards, 2)]
    near = [swap(x, "dp", 1) for x in [pack] + far]
    mixer_shards = [x for pair in zip([pack] + far, near) for x in pair]
    def second_pack(filler):
        return jnp.concatenate([w_gate, w_up, w_down.T, filler[:depth, : FF_PAD - ff]], axis=1)

    pack_two = second_pack(far[-1])
    steps_two = list(range(2, shards, 2))
    far_two = [swap(pack_two, "dp", k) for k in steps_two[:-1]]
    one, two = ORDER
    near_two = [swap(pack_two, "dp", 1)]
    out = mixer_fwd(me, ends, flat, count, 0, shards=mixer_shards)
    fwd = [list(out[:10]) + [out[14], width // STEP]]
    w_in, small = out[10], (out[11], out[12])
    pack_late = second_pack(out[4])
    head_far = swap(out[4], "mp", 2)
    head_near = swap(out[4], "mp", 1)
    near_two += [swap(x, "dp", 1) for x in far_two]
    far_two.append(swap(pack_late, "dp", steps_two[-1]))
    carried = out[13:]
    out = mixer_fwd(
        me, ends, flat, count, count, after=far_two[:-1] + near_two[:1], w_in=w_in, small=small, carried=carried
    )
    fwd.append(list(out[:10]) + [carried[1], 0])
    own = gate(out[4], [head_far, head_near, far_two[-1]] + near_two[1:])
    fwd[1][4] = own
    near_two.append(swap(far_two[-1], "dp", 1))
    mlp_shards = [x for pair in zip([pack_two] + far_two, near_two) for x in pair]
    far_heads = swap(own, "mp", 2)
    heads = [
        [fwd[0][4], head_near, head_far, swap(head_far, "mp", 1)],
        [own, swap(own, "mp", 1), far_heads, swap(far_heads, "mp", 1)],
    ]
    wo_own = fwd[0][4]
    mid = {}
    out = mlp(
        me, flat, cot, small, heads[one], fwd[one][11], count, one * count, ff, shards=mlp_shards, wo=heads[0],
        after=heads[two][1:],
    )
    weights, mid[one] = list(out[10:]), out[:10]
    p_one = pair_sum(out[0], swap(out[1], "mp", 1))
    q_one = swap(p_one, "mp", 2)
    down_one = swap(out[3], "mp", 1)
    out = mlp(me, flat, cot, small, heads[two], fwd[two][11], count, two * count, ff, after=[p_one], weights=weights)
    mid[two] = out
    p_two = pair_sum(out[0], swap(gate(out[1], [q_one, down_one]), "mp", 1))
    q_two = swap(p_two, "mp", 2)
    down_two = swap(out[3], "mp", 1)
    s_one = p_one + q_one
    s_one_other = swap(s_one, "mp", 1)
    chunks = (one, two)
    same_a, other_a = mlp_grads(
        me, [mid[c][5] for c in chunks], [0] * CHUNKS, [mid[c][7] for c in chunks] + [mid[c][8] for c in chunks],
        shards, ff, after=[p_two, s_one],
    )
    same_b, other_b = mlp_grads(
        me, [cot] * CHUNKS, chunks, [mid[c][6] for c in chunks], shards, ff, after=[same_a],
    )
    s_two = pair_after(p_two, q_two, [same_b, s_one_other, down_one, down_two])
    s_two_other = swap(s_two, "mp", 1)
    down_one = pair_after(mid[one][2], down_one, [s_two])
    far_one = swap(down_one, "mp", 2)
    down_parts = split_pair_after(mid[two][2], down_two, [down_one])
    far_part = swap(down_parts[0], "mp", 2)
    other_a = swap(other_a, "dp", 1)
    other_b = swap(other_b, "dp", 1)
    out_one = mixer_bwd(
        me, ends, s_one, s_one_other, mid[one][4], cot, flat, fwd[one], w_in, wo_own, small, one * count, None, False,
        shards, after=[down_parts[0]],
    )
    other_a, other_b = gate(other_a, [out_one[0]]), gate(other_b, [out_one[0]])
    n_one = pair_sum(out_one[0], swap(gate(out_one[1], [far_one, far_part, other_a, other_b, s_two_other]), "mp", 1))
    m_one = swap(n_one, "mp", 2)
    far_parts = [far_part, swap(gate(down_parts[1], [n_one]), "mp", 2)]
    half = shards // 4
    same_a, other_a = same_a[:half] + other_a[:half], same_a[half:] + other_a[half:]
    other_a = swap(other_a, "dp", 2)
    same_b, other_b = same_b[:half] + other_b[:half], same_b[half:] + other_b[half:]
    other_b = swap(other_b, "dp", 2)
    out_two = mixer_bwd(
        me, ends, s_two, s_two_other, mid[two][4], cot, flat, fwd[two], w_in, wo_own, small, two * count,
        list(out_one[3:]), True, shards, after=[n_one, same_a, same_b], ggain=(mid[one][9], mid[two][9]),
    )
    other_mix = swap(out_two[4], "dp", 1)
    n_theirs = gate(out_two[1], [m_one, far_parts[1], other_a, other_b])
    sum_a, sum_b = finish(same_a, other_a, 2), finish(same_b, other_b, 2)
    n_two = pair_after(out_two[0], swap(n_theirs, "mp", 1), [sum_a[2], sum_b[2]])
    m_two = swap(n_two, "mp", 2)
    layer_out = token_grad = None
    sent = jnp.concatenate([d + f for d, f in zip(down_parts, far_parts)], axis=0)
    for c, sent in ((one, down_one + far_one), (two, sent)):
        layer_out = final(me, sent, swap(sent, "mp", 1), mid[c][4], flat, small[0], c * count, BF, layer_out)
    sent = n_one + m_one
    token_grad = final(me, sent, swap(sent, "mp", 1), out_one[2], flat, small[0], one * count, F32, None)
    other_mix = gate(other_mix, [m_two, layer_out, token_grad, sum_a[1], sum_b[1]])
    sent = n_two + m_two
    token_grad = final(me, sent, swap(sent, "mp", 1), out_two[2], flat, small[0], two * count, F32, token_grad)
    sum_a = last_sum(sum_a[0], gate(sum_a[1], [m_two]))
    sum_b = last_sum(sum_b[0], gate(sum_b[1], [m_two]))
    mix_same, mix_other, _ = finish(out_two[3], other_mix, 1, [token_grad, sum_a, sum_b])
    mix_sum = last_sum(mix_same, mix_other)
    extra = mix_sum[:, 768:896]
    gains = jnp.concatenate([extra[:, 2], extra[:, 3], extra[:each, HEAD_ROW]])
    gains = (gains + swap(gains, "mp", 1)) + (swap(gains, "mp", 2) + swap(gains, "mp", 3))
    return (
        layer_out.reshape(seq_rows, length, width),
        token_grad.reshape(seq_rows, length, width),
        gains[:depth],
        mix_sum[:, 0:256],
        mix_sum[:, 256:512],
        mix_sum[:, 512:768],
        extra[:, 0:2],
        extra[:each, TAP_ROW:HEAD_ROW].T.reshape(2, 12, each),
        gains[2 * depth :],
        mix_sum[:, 896:1152].T,
        gains[depth : 2 * depth],
        sum_a[:, :ff],
        sum_a[:, ff : 2 * ff],
        sum_b[:, :ff].T,
    )


def solution(mesh):
    return jax.shard_map(
        on_device,
        mesh=mesh,
        in_specs=(
            P("dp", None, None),
            P("dp", None),
            P("dp", None, None),
            P("dp"),
            P("dp", "mp"),
            P("dp", "mp"),
            P("dp", "mp"),
            P("dp", "mp"),
            P("mp", None, "dp"),
            P("dp"),
            P("mp", "dp"),
            P("dp"),
            P("dp", "mp"),
            P("dp", "mp"),
            P("mp", "dp"),
        ),
        out_specs=(
            P("dp", None, None),
            P("dp", None, None),
            P("dp"),
            P("dp", "mp"),
            P("dp", "mp"),
            P("dp", "mp"),
            P("dp", "mp"),
            P("mp", None, "dp"),
            P("dp"),
            P("mp", "dp"),
            P("dp"),
            P("dp", "mp"),
            P("dp", "mp"),
            P("mp", "dp"),
        ),
        check_vma=False,
    )
```
